128 devices in a mesh: dp: 64 (over y, z, x), split: 2 (over core).
Axes of the slice: x: 4, y: 4, z: 4, core: 2. Of those that a mesh axis runs over, the one named last changes fastest.
Arguments:
- embeddings: bfloat16 [131072, 768], P(('dp', 'split')), may hold values from -6 to 6
- cluster: int32 [131072], P(('dp', 'split')), may hold values from 0 to 511, as said below
- rank: int32 [131072], P(('dp', 'split')), may hold values from 0 to 131071, each once
Outputs:
- max_cosine: float32 [131072], P(('dp', 'split'))
The draws below stay inside these ranges and needn't reach their ends.
Inputs may be any that keep to these rules, and one draw needn't show every extreme that they name: cluster // 8 names the row's owner, an index of dp. The rows of one device name each owner at most 32 times, and in every draw one owner is named exactly 32 times by the rows of every device.
All inputs are finite; a program needn't handle non-finite values.
Results may differ from the reference program's by a relative error of at most 0.0014.
Values may be sent and summed in bfloat16 or wider, within the bound.
A program may use at most 64 MiB of HBM per device.

```python
import jax
import jax.numpy as jnp
from jax import lax

D = 768
TOK_DEV = 1024
CL_DEV = 8
CAP = 32
ROWS = 131072
N_DP = 64
N_SPLIT = 2


def draw_cluster(key, part):
    key = jax.random.fold_in(key, 11)
    key_full, key_blocks = jax.random.split(key)
    full_owner = jax.random.randint(key_full, (), 0, N_DP)
    blocks = ROWS // TOK_DEV

    def one_block(block_key):
        key_pick, key_mix, key_within = jax.random.split(block_key, 3)
        others = (jnp.arange((N_DP - 1) * CAP, dtype=jnp.int32) // CAP + full_owner + 1) % N_DP
        chosen = jax.random.permutation(key_pick, others)[:TOK_DEV - CAP]
        labels = jnp.concatenate([jnp.full((CAP,), full_owner, jnp.int32), chosen.astype(jnp.int32)])
        labels = jax.random.permutation(key_mix, labels)
        within = jax.random.randint(key_within, (TOK_DEV,), 0, CL_DEV)
        return labels * CL_DEV + within
    return jax.vmap(one_block)(jax.random.split(key_blocks, blocks)).reshape(ROWS).astype(jnp.int32)


def block_levels(key, extent, shards, low, high):
    def one(axis_at, blocks):
        steps = jax.random.uniform(jax.random.fold_in(jax.random.fold_in(key, 6), axis_at), (blocks,), jnp.float32, low / len(shards), high / len(shards))
        return jnp.repeat(jnp.exp(steps), extent[axis_at] // blocks).reshape((-1,) + (1,) * (len(extent) - axis_at - 1))

    gain = one(*shards[0])
    for cut in shards[1:]:
        gain = gain * one(*cut)
    return gain


def centred(rng, dims, scale, limit, shards=(), kind=jnp.bfloat16):
    result = jax.random.normal(rng, dims, jnp.float32) * scale
    if len(shards) > 0:
        result = block_levels(rng, dims, shards, -0.22, 0.18) * result
    return jnp.clip(result, min=-limit, max=limit).astype(kind)


def setup_inputs(seed: int = 0) -> dict:
    key_list = jax.random.split(jax.random.key(seed), 4)
    embeddings = centred(key_list[0], (ROWS, D), 1.0, 6.0, ((0, 128),))
    cluster = draw_cluster(jax.random.fold_in(key_list[3], 71), 0)
    rank = jax.random.permutation(key_list[2], ROWS).astype(jnp.int32)
    return dict(embeddings=embeddings, cluster=cluster, rank=rank)


def reference(embeddings, cluster, rank):
    values = embeddings.astype(jnp.float32)
    unit = (values * lax.rsqrt(lax.optimization_barrier(jnp.sum(values * values, axis=1, keepdims=True)) + 1e-06)).astype(jnp.bfloat16)
    order = jnp.argsort(cluster * ROWS + rank).astype(jnp.int32)
    sorted_unit = unit[order]
    sorted_cluster = cluster[order]
    sorted_rank = rank[order]
    window = N_DP * N_SPLIT * CAP
    block = 512
    padded_unit = jnp.concatenate([jnp.zeros((window, D), jnp.bfloat16), sorted_unit], axis=0)
    padded_cluster = jnp.concatenate([jnp.full((window,), -1, jnp.int32), sorted_cluster.astype(jnp.int32)])
    padded_rank = jnp.concatenate([jnp.zeros((window,), jnp.int32), sorted_rank.astype(jnp.int32)])

    def one_block(index):
        start = (index * block).astype(jnp.int32)
        queries = lax.dynamic_slice_in_dim(sorted_unit, start, block, 0)
        query_cluster = lax.dynamic_slice_in_dim(sorted_cluster, start, block, 0)
        query_rank = lax.dynamic_slice_in_dim(sorted_rank, start, block, 0)
        keys = lax.dynamic_slice_in_dim(padded_unit, start, window + block, 0)
        key_cluster = lax.dynamic_slice_in_dim(padded_cluster, start, window + block, 0)
        key_rank = lax.dynamic_slice_in_dim(padded_rank, start, window + block, 0)
        scores = lax.dot_general(queries, keys, (((1,), (1,)), ((), ())), preferred_element_type=jnp.float32)
        allowed = (query_cluster[:, None] == key_cluster[None, :]) & (key_rank[None, :] < query_rank[:, None]) & (key_cluster[None, :] >= 0)
        return lax.optimization_barrier(jnp.max(jnp.where(allowed, scores, jnp.float32(-1.0)), axis=1))
    results = lax.map(one_block, jnp.arange(ROWS // block, dtype=jnp.int32)).reshape(ROWS)
    return jnp.zeros((ROWS,), jnp.float32).at[order].set(results)
```

```python
import jax
import jax.numpy as jnp
from jax import lax
from jax.experimental import pallas as pl
from jax.experimental.pallas import tpu as pltpu
from jax.sharding import PartitionSpec as P

MESH = pl.DeviceIdType.MESH
OWNERS = 64
CAP = 32
ROWS = 1024
D = 768
RANKS = 131072
GROUP = 8
GROUPS = OWNERS // GROUP
WIDE = GROUP * CAP
EMPTY = 16777216.0


def link_load(step):
    load = []
    for part in step:
        load += [1 if part in (1, 2) else 0, 1 if part in (3, 2) else 0]
    return load


def balanced_order():
    left = [
        (index // 16, index // 4 % 4, index % 4)
        for index in sorted(range(1, OWNERS), key=lambda index: index * 37 % 64)
    ]
    total = [0] * 6
    order = [(0, 0, 0)]

    def score(step):
        sums = [a + b for a, b in zip(total, link_load(step))]
        return max(sums) - min(sums), -sum(min(part, 4 - part) for part in step)

    while left:
        best = min(left, key=score)
        left.remove(best)
        order.append(best)
        total = [a + b for a, b in zip(total, link_load(best))]
    return order


ORDER = balanced_order()


def nt_dot(a, b):
    return lax.dot_general(a, b, (((1,), (1,)), ((), ())), preferred_element_type=jnp.float32)


def kernel(
    emb_hbm, cluster_hbm, rank_hbm, out_ref,
    emb, cluster, rank, unit, hits, place, sel, picks,
    send_rows, own_rows, far_rows, send_codes, own_codes, far_codes,
    own_keys, far_keys, limits, best, send_back, got_back,
    load_sem, row_send, row_recv, code_send, code_recv, far_send, far_recv, back_send, back_recv,
):
    me = lax.axis_index("dp")
    core = lax.axis_index("split")
    my, mz, mx = me // 16, me // 4 % 4, me % 4

    def peer(step, sign):
        y = (my + sign * step[0] + 4) % 4
        z = (mz + sign * step[1] + 4) % 4
        x = (mx + sign * step[2] + 4) % 4
        return (y * 16 + z * 4 + x, core)

    sibling = (me, 1 - core)

    loads = [
        pltpu.make_async_copy(source, target, load_sem.at[index])
        for index, (source, target) in enumerate(
            ((cluster_hbm, cluster), (rank_hbm, rank), (emb_hbm, emb))
        )
    ]
    for load in loads:
        load.start()
    barrier = pltpu.get_barrier_semaphore()
    for step in ORDER[1:]:
        pl.semaphore_signal(barrier, inc=1, device_id=peer(step, 1), device_id_type=MESH)
    pl.semaphore_signal(barrier, inc=1, device_id=sibling, device_id_type=MESH)

    loads[0].wait()
    loads[1].wait()
    slot = lax.broadcasted_iota(jnp.int32, (OWNERS, 128), 0)
    route = jnp.zeros((OWNERS, 128), jnp.int32)
    for index, step in enumerate(ORDER):
        route = jnp.where(slot == index, step[0] * 16 + step[1] * 4 + step[2], route)
    digits = []
    for tile in range(8):
        ids = cluster[tile : tile + 1, :]
        owner = ids // 8
        step_y = (owner // 16 - my + 4) % 4
        step_z = (owner // 4 % 4 - mz + 4) % 4
        step_x = (owner % 4 - mx + 4) % 4
        code = step_y * 16 + step_z * 4 + step_x
        hit = jnp.where(route == code, 1.0, 0.0)
        hits[:, tile * 128 : (tile + 1) * 128] = hit.astype(jnp.bfloat16)
        code = ids % 8 * RANKS + rank[tile : tile + 1, :] + 1
        digits.append((code % 256, code // 256 % 256, code // 65536))
    lower = lax.broadcasted_iota(jnp.int32, (256, 256), 0)
    upper = lax.broadcasted_iota(jnp.int32, (256, 256), 1)
    before = jnp.where(lower <= upper, 1.0, 0.0).astype(jnp.bfloat16)
    carry = jnp.zeros((OWNERS, 1), jnp.float32)
    for part in range(4):
        cols = slice(part * 256, (part + 1) * 256)
        count = jnp.dot(hits[:, cols], before, preferred_element_type=jnp.float32) + carry
        carry = count[:, 255:256]
        place[:, cols] = jnp.where(hits[:, cols].astype(jnp.float32) > 0.5, count, 0.0)
    digit = jnp.concatenate(
        [jnp.concatenate([piece[row] for piece in digits], axis=1) for row in range(3)]
        + [jnp.zeros((5, ROWS), jnp.int32)],
        axis=0,
    )
    digit = digit.astype(jnp.float32).astype(jnp.bfloat16)

    loads[2].wait()

    def normalise(index, _):
        rows = pl.ds(pl.multiple_of(index * 128, 128), 128)
        values = emb[rows, :].astype(jnp.float32)
        total = jnp.sum(values * values, axis=1, keepdims=True)
        unit[rows, :] = (values * lax.rsqrt(total + 1e-06)).astype(jnp.bfloat16)
        return 0

    lax.fori_loop(0, 8, normalise, 0)

    spot = lax.broadcasted_iota(jnp.int32, (CAP, ROWS), 0).astype(jnp.float32) + 1.0
    row_copies, code_copies = [], []
    for group in range(GROUPS):
        for index in range(GROUP):
            line = place[group * GROUP + index : group * GROUP + index + 1, :]
            chosen = jnp.where(jnp.broadcast_to(line, (CAP, ROWS)) == spot, 1.0, 0.0)
            sel[index * CAP : (index + 1) * CAP, :] = chosen.astype(jnp.bfloat16)
        picked = jnp.dot(sel[...], unit[...], preferred_element_type=jnp.float32)
        picked = picked.astype(jnp.bfloat16).reshape(GROUP, CAP, D)
        send_rows[group * GROUP : (group + 1) * GROUP] = picked
        parts = nt_dot(digit, sel[...])
        codes = parts[0:1] + parts[1:2] * 256.0 + parts[2:3] * 65536.0
        for index in range(GROUP):
            half = index // 4 * 128
            send_codes[group * GROUP + index] = codes[:, half : half + 128]
        if group == 0:
            own_rows[0] = picked[0]
            own_codes[0] = codes[:, 0:128]
            pl.semaphore_wait(barrier, OWNERS)
        for index in range(max(1, group * GROUP), (group + 1) * GROUP):
            target = peer(ORDER[index], 1)
            copy = pltpu.make_async_remote_copy(
                src_ref=send_codes.at[index], dst_ref=own_codes.at[index],
                send_sem=code_send, recv_sem=code_recv,
                device_id=target, device_id_type=MESH,
            )
            copy.start()
            copy = pltpu.make_async_remote_copy(
                src_ref=send_rows.at[index], dst_ref=own_rows.at[index],
                send_sem=row_send, recv_sem=row_recv.at[group],
                device_id=target, device_id_type=MESH,
            )
            copy.start()

    turn = lax.broadcasted_iota(jnp.int32, (OWNERS, ROWS), 0) % 4 * CAP
    where = jnp.where(place[...] > 0.5, place[...] - 1.0 + turn.astype(jnp.float32), 0.0)
    where = jnp.sum(where, axis=0, keepdims=True)
    lane = lax.broadcasted_iota(jnp.int32, (128, ROWS), 0).astype(jnp.float32)
    picks[...] = jnp.where(lane == where, 1.0, 0.0).astype(jnp.bfloat16)

    def spread(codes, keys, is_own):
        block = codes[...].reshape(OWNERS // 4, 4, 1, 128)
        part = lax.broadcasted_iota(jnp.int32, block.shape, 1)
        at = lax.broadcasted_iota(jnp.int32, block.shape, 3) // CAP
        line = jnp.sum(jnp.where(part == at, block, 0.0), axis=1)
        if is_own:
            limits[0] = line
            limits[1] = jnp.floor((line - 1.0) * (1.0 / RANKS)) * float(RANKS) + 1.0
        line = jnp.where(line == 0.0, EMPTY, line)
        for index in range(OWNERS // 4):
            square = jnp.broadcast_to(line[index], (128, 128))
            keys[index * 128 : (index + 1) * 128, :] = square.T

    pltpu.make_async_copy(own_codes.at[1:], own_codes.at[1:], code_recv).wait()
    code_hop = pltpu.make_async_remote_copy(
        src_ref=own_codes, dst_ref=far_codes,
        send_sem=far_send.at[GROUPS], recv_sem=far_recv.at[GROUPS],
        device_id=sibling, device_id_type=MESH,
    )
    code_hop.start()
    spread(own_codes, own_keys, True)
    best[...] = jnp.full(best.shape, -1.0, jnp.float32)

    def compare(query, blocks):
        at = pl.multiple_of(query * GROUP, GROUP)
        rows = own_rows[pl.ds(at, GROUP)].reshape(WIDE, D)
        high = limits[0, pl.ds(query * 2, 2)]
        low = limits[1, pl.ds(query * 2, 2)]
        tops = [best[query, :, half * 128 : (half + 1) * 128] for half in range(2)]
        for data, keys, block in blocks:
            key_at = pl.multiple_of(block * GROUP, GROUP)
            scores = nt_dot(data[pl.ds(key_at, GROUP)].reshape(WIDE, D), rows)
            code = keys[pl.ds(pl.multiple_of(block * WIDE, WIDE), WIDE), :]
            for half in range(2):
                allowed = (code < high[half]) & (code >= low[half])
                part = scores[:, half * 128 : (half + 1) * 128]
                part = jnp.where(allowed, part, -1.0).reshape(WIDE // 8, 8, 128)
                tops[half] = jnp.maximum(tops[half], jnp.max(part, axis=0))
        for half in range(2):
            best[query, :, half * 128 : (half + 1) * 128] = tops[half]

    hops = []
    for step in range(GROUPS + 1):
        if step < GROUPS:
            here = own_rows.at[max(1, step * GROUP) : (step + 1) * GROUP]
            pltpu.make_async_copy(here, here, row_recv.at[step]).wait()
            block = pl.ds(step * GROUP, GROUP)
            hop = pltpu.make_async_remote_copy(
                src_ref=own_rows.at[block], dst_ref=far_rows.at[block],
                send_sem=far_send.at[step], recv_sem=far_recv.at[step],
                device_id=sibling, device_id_type=MESH,
            )
            hop.start()
            hops.append(hop)
        fresh = []
        if step < GROUPS:
            fresh.append((own_rows, own_keys, step))
        if step == 0:
            code_hop.wait_recv()
            spread(far_codes, far_keys, False)
        else:
            hops[step - 1].wait_recv()
            fresh.append((far_rows, far_keys, step - 1))

        def old_queries(query, _, fresh=fresh):
            compare(query, fresh)
            return 0

        if step < GROUPS:
            lax.fori_loop(0, step, old_queries, 0)

            def old_keys(block, _, step=step):
                compare(step, [(own_rows, own_keys, block), (far_rows, far_keys, block)])
                return 0

            lax.fori_loop(0, step, old_keys, 0)
            compare(step, [(own_rows, own_keys, step)])
        else:
            for query in range(GROUPS):
                compare(query, fresh)
                for half in range(2):
                    top = jnp.max(best[query, :, half * 128 : (half + 1) * 128], axis=0, keepdims=True)
                    send_back[query * 2 + half] = top
                for index in range(query * GROUP, (query + 1) * GROUP):
                    if index == 0:
                        got_back[0] = send_back[0]
                        continue
                    copy = pltpu.make_async_remote_copy(
                        src_ref=send_back.at[index // 4], dst_ref=got_back.at[index],
                        send_sem=back_send, recv_sem=back_recv,
                        device_id=peer(ORDER[index], -1), device_id_type=MESH,
                    )
                    copy.start()

    pltpu.make_async_copy(got_back.at[1:], got_back.at[1:], back_recv).wait()
    back = got_back[...].reshape(OWNERS, 128)
    first = back.astype(jnp.bfloat16)
    rest = back - first.astype(jnp.float32)
    second = rest.astype(jnp.bfloat16)
    third = (rest - second.astype(jnp.float32)).astype(jnp.bfloat16)
    moved = [
        jnp.dot(piece, picks[...], preferred_element_type=jnp.float32)
        for piece in (first, second, third)
    ]
    moved = moved[0] + moved[1] + moved[2]
    result = jnp.sum(jnp.where(place[...] > 0.5, moved, 0.0), axis=0, keepdims=True)
    for tile in range(8):
        out_ref[tile : tile + 1, :] = result[:, tile * 128 : (tile + 1) * 128]

    pltpu.make_async_copy(send_rows.at[1:], send_rows.at[1:], row_send).wait()
    pltpu.make_async_copy(send_codes.at[1:], send_codes.at[1:], code_send).wait()
    pltpu.make_async_copy(got_back.at[1:], got_back.at[1:], back_send).wait()
    code_hop.wait_send()
    for hop in hops:
        hop.wait_send()


def shards(embeddings, cluster, rank):
    rows = (OWNERS, CAP, D)
    codes = (OWNERS, 1, 128)
    f32, bf16 = jnp.float32, jnp.bfloat16
    dma = pltpu.SemaphoreType.DMA
    result = pl.pallas_call(
        kernel,
        out_shape=jax.ShapeDtypeStruct((8, 128), f32),
        in_specs=[pl.BlockSpec(memory_space=pltpu.HBM)] * 3,
        out_specs=pl.BlockSpec(memory_space=pltpu.VMEM),
        scratch_shapes=[
            pltpu.VMEM((ROWS, D), bf16),
            pltpu.VMEM((8, 128), jnp.int32),
            pltpu.VMEM((8, 128), jnp.int32),
            pltpu.VMEM((ROWS, D), bf16),
            pltpu.VMEM((OWNERS, ROWS), bf16),
            pltpu.VMEM((OWNERS, ROWS), f32),
            pltpu.VMEM((WIDE, ROWS), bf16),
            pltpu.VMEM((128, ROWS), bf16),
            pltpu.VMEM(rows, bf16),
            pltpu.VMEM(rows, bf16),
            pltpu.VMEM(rows, bf16),
            pltpu.VMEM(codes, f32),
            pltpu.VMEM(codes, f32),
            pltpu.VMEM(codes, f32),
            pltpu.VMEM((OWNERS * CAP, 128), f32),
            pltpu.VMEM((OWNERS * CAP, 128), f32),
            pltpu.VMEM((2, OWNERS // 4, 1, 128), f32),
            pltpu.VMEM((GROUPS, 8, WIDE), f32),
            pltpu.VMEM((OWNERS // 4, 1, 128), f32),
            pltpu.VMEM(codes, f32),
            dma((3,)),
            dma,
            dma((GROUPS,)),
            dma,
            dma,
            dma((GROUPS + 1,)),
            dma((GROUPS + 1,)),
            dma,
            dma,
        ],
        compiler_params=pltpu.CompilerParams(
            collective_id=0, has_side_effects=True, vmem_limit_bytes=40 * 2**20
        ),
        cost_estimate=pl.CostEstimate(
            flops=2 * D * 2048 * (4096 + 1024), bytes_accessed=2 * ROWS * D, transcendentals=ROWS
        ),
        name="dedup",
    )(embeddings, cluster.reshape(8, 128), rank.reshape(8, 128))
    return result.reshape(ROWS)


def solution(mesh):
    in_specs = (P(("dp", "split"), None), P(("dp", "split")), P(("dp", "split")))
    out_specs = P(("dp", "split"))
    return jax.shard_map(shards, mesh=mesh, in_specs=in_specs, out_specs=out_specs, check_vma=False)
```

```python
import jax
import jax.numpy as jnp
from jax import lax
from jax.experimental import pallas as pl
from jax.experimental.pallas import tpu as pltpu
from jax.sharding import PartitionSpec as P

MESH = pl.DeviceIdType.MESH
OWNERS = 64
CAP = 32
ROWS = 1024
D = 768
RANKS = 131072
GROUP = 8
GROUPS = OWNERS // GROUP
WIDE = GROUP * CAP
EMPTY = 16777216.0
STRAIGHT = 4


def link_load(step):
    load = []
    for part in step:
        load += [1 if part in (1, 2) else 0, 1 if part in (3, 2) else 0]
    return load


def balanced_order():
    left = [
        (index // 16, index // 4 % 4, index % 4)
        for index in sorted(range(1, OWNERS), key=lambda index: index * 37 % 64)
    ]
    total = [0] * 6
    order = [(0, 0, 0)]

    def score(step):
        sums = [a + b for a, b in zip(total, link_load(step))]
        return max(sums) - min(sums), -sum(min(part, 4 - part) for part in step)

    while left:
        best = min(left, key=score)
        left.remove(best)
        order.append(best)
        total = [a + b for a, b in zip(total, link_load(best))]
    return order


ORDER = balanced_order()


def nt_dot(a, b):
    return lax.dot_general(a, b, (((1,), (1,)), ((), ())), preferred_element_type=jnp.float32)


def kernel(
    emb_hbm, cluster_hbm, rank_hbm, out_ref,
    emb, cluster, rank, unit, hits, place, sel, picks,
    send_rows, own_rows, far_rows, send_codes, own_codes, far_codes,
    own_keys, far_keys, limits, best, send_back, got_back,
    load_sem, row_send, row_recv, code_send, code_recv, far_send, far_recv, back_send, back_recv,
):
    me = lax.axis_index("dp")
    core = lax.axis_index("split")
    my, mz, mx = me // 16, me // 4 % 4, me % 4

    def peer(step, sign):
        y = (my + sign * step[0] + 4) % 4
        z = (mz + sign * step[1] + 4) % 4
        x = (mx + sign * step[2] + 4) % 4
        return (y * 16 + z * 4 + x, core)

    sibling = (me, 1 - core)

    loads = [
        pltpu.make_async_copy(source, target, load_sem.at[index])
        for index, (source, target) in enumerate(
            ((cluster_hbm, cluster), (rank_hbm, rank), (emb_hbm, emb))
        )
    ]
    for load in loads:
        load.start()
    barrier = pltpu.get_barrier_semaphore()
    for step in ORDER[1:]:
        pl.semaphore_signal(barrier, inc=1, device_id=peer(step, 1), device_id_type=MESH)
    pl.semaphore_signal(barrier, inc=1, device_id=sibling, device_id_type=MESH)

    loads[0].wait()
    loads[1].wait()
    slot = lax.broadcasted_iota(jnp.int32, (OWNERS, 128), 0)
    route = jnp.zeros((OWNERS, 128), jnp.int32)
    for index, step in enumerate(ORDER):
        route = jnp.where(slot == index, step[0] * 16 + step[1] * 4 + step[2], route)
    words = []
    for tile in range(8):
        ids = cluster[tile : tile + 1, :]
        owner = ids // 8
        step_y = (owner // 16 - my + 4) % 4
        step_z = (owner // 4 % 4 - mz + 4) % 4
        step_x = (owner % 4 - mx + 4) % 4
        code = step_y * 16 + step_z * 4 + step_x
        hit = jnp.where(route == code, 1.0, 0.0)
        hits[:, tile * 128 : (tile + 1) * 128] = hit.astype(jnp.bfloat16)
        words.append(ids % 8 * RANKS + rank[tile : tile + 1, :] + 1)
    lower = lax.broadcasted_iota(jnp.int32, (256, 256), 0)
    upper = lax.broadcasted_iota(jnp.int32, (256, 256), 1)
    before = jnp.where(lower <= upper, 1.0, 0.0).astype(jnp.bfloat16)
    carry = jnp.zeros((OWNERS, 1), jnp.float32)
    for part in range(4):
        cols = slice(part * 256, (part + 1) * 256)
        count = jnp.dot(hits[:, cols], before, preferred_element_type=jnp.float32) + carry
        carry = count[:, 255:256]
        place[:, cols] = jnp.where(hits[:, cols].astype(jnp.float32) > 0.5, count, 0.0)
    turn = lax.broadcasted_iota(jnp.int32, (OWNERS, ROWS), 0) % 4 * CAP
    where = jnp.where(place[...] > 0.5, place[...] - 1.0 + turn.astype(jnp.float32), 0.0)
    where = jnp.sum(where, axis=0, keepdims=True)
    lane = lax.broadcasted_iota(jnp.int32, (128, ROWS), 0).astype(jnp.float32)
    picks[...] = jnp.where(lane == where, 1.0, 0.0).astype(jnp.bfloat16)

    word = jnp.concatenate(words, axis=1)
    codes = jnp.zeros((OWNERS, 128), jnp.float32)
    for power, digit in ((1, word % 256), (256, word // 256 % 256), (65536, word // 65536)):
        marked = hits[...] * digit.astype(jnp.float32).astype(jnp.bfloat16)
        codes = codes + nt_dot(marked, picks[...]) * float(power)
    send_codes[...] = codes.reshape(OWNERS, 1, 128)
    own_codes[0] = send_codes[0]
    pl.semaphore_wait(barrier, OWNERS)
    for index in range(1, OWNERS):
        copy = pltpu.make_async_remote_copy(
            src_ref=send_codes.at[index], dst_ref=own_codes.at[index],
            send_sem=code_send, recv_sem=code_recv,
            device_id=peer(ORDER[index], 1), device_id_type=MESH,
        )
        copy.start()

    loads[2].wait()

    def normalise(index, _):
        rows = pl.ds(pl.multiple_of(index * 128, 128), 128)
        values = emb[rows, :].astype(jnp.float32)
        total = jnp.sum(values * values, axis=1, keepdims=True)
        unit[rows, :] = (values * lax.rsqrt(total + 1e-06)).astype(jnp.bfloat16)
        return 0

    lax.fori_loop(0, 8, normalise, 0)

    spot = lax.broadcasted_iota(jnp.int32, (CAP, ROWS), 0).astype(jnp.float32) + 1.0
    for group in range(GROUPS):
        for index in range(GROUP):
            line = place[group * GROUP + index : group * GROUP + index + 1, :]
            chosen = jnp.where(jnp.broadcast_to(line, (CAP, ROWS)) == spot, 1.0, 0.0)
            sel[index * CAP : (index + 1) * CAP, :] = chosen.astype(jnp.bfloat16)
        picked = jnp.dot(sel[...], unit[...], preferred_element_type=jnp.float32)
        picked = picked.astype(jnp.bfloat16).reshape(GROUP, CAP, D)
        send_rows[group * GROUP : (group + 1) * GROUP] = picked
        if group == 0:
            own_rows[0] = picked[0]
        for index in range(max(1, group * GROUP), (group + 1) * GROUP):
            target = peer(ORDER[index], 1)
            copy = pltpu.make_async_remote_copy(
                src_ref=send_rows.at[index], dst_ref=own_rows.at[index],
                send_sem=row_send, recv_sem=row_recv.at[group],
                device_id=target, device_id_type=MESH,
            )
            copy.start()

    def spread(codes, keys, is_own):
        block = codes[...].reshape(OWNERS // 4, 4, 1, 128)
        line = jnp.sum(block, axis=1)
        if is_own:
            limits[0] = line
            limits[1] = jnp.floor((line - 1.0) * (1.0 / RANKS)) * float(RANKS) + 1.0
        line = jnp.where(line == 0.0, EMPTY, line)
        for index in range(OWNERS // 4):
            square = jnp.broadcast_to(line[index], (128, 128))
            keys[index * 128 : (index + 1) * 128, :] = square.T

    pltpu.make_async_copy(own_codes.at[1:], own_codes.at[1:], code_recv).wait()
    code_hop = pltpu.make_async_remote_copy(
        src_ref=own_codes, dst_ref=far_codes,
        send_sem=far_send.at[GROUPS], recv_sem=far_recv.at[GROUPS],
        device_id=sibling, device_id_type=MESH,
    )
    code_hop.start()
    spread(own_codes, own_keys, True)
    best[...] = jnp.full(best.shape, -1.0, jnp.float32)

    def compare(query, blocks):
        start = query * GROUP
        if not isinstance(query, int):
            start = pl.multiple_of(start, GROUP)
        rows = own_rows[pl.ds(start, GROUP)].reshape(WIDE, D)
        high = limits[0, pl.ds(query * 2, 2)]
        low = limits[1, pl.ds(query * 2, 2)]
        tops = [best[query, :, half * 128 : (half + 1) * 128] for half in range(2)]
        for data, keys, block in blocks:
            start, slots = block * GROUP, block * WIDE
            if not isinstance(block, int):
                start, slots = pl.multiple_of(start, GROUP), pl.multiple_of(slots, WIDE)
            scores = nt_dot(data[pl.ds(start, GROUP)].reshape(WIDE, D), rows)
            code = keys[pl.ds(slots, WIDE), :]
            for half in range(2):
                allowed = (code < high[half]) & (code >= low[half])
                part = scores[:, half * 128 : (half + 1) * 128]
                part = jnp.where(allowed, part, -1.0).reshape(WIDE // 8, 8, 128)
                tops[half] = jnp.maximum(tops[half], jnp.max(part, axis=0))
        for half in range(2):
            best[query, :, half * 128 : (half + 1) * 128] = tops[half]

    hops = []
    for step in range(GROUPS):
        here = own_rows.at[max(1, step * GROUP) : (step + 1) * GROUP]
        pltpu.make_async_copy(here, here, row_recv.at[step]).wait()
        block = pl.ds(step * GROUP, GROUP)
        hop = pltpu.make_async_remote_copy(
            src_ref=own_rows.at[block], dst_ref=far_rows.at[block],
            send_sem=far_send.at[step], recv_sem=far_recv.at[step],
            device_id=sibling, device_id_type=MESH,
        )
        hop.start()
        hops.append(hop)
        own_block, far_block = (own_rows, own_keys, step), (far_rows, far_keys, step)
        if step < STRAIGHT:

            def earlier(block, _, step=step, own_block=own_block):
                compare(block, [own_block])
                compare(step, [(own_rows, own_keys, block), (far_rows, far_keys, block)])
                return 0

            lax.fori_loop(0, step, earlier, 0)
            compare(step, [own_block])
        else:
            for query in range(step):
                compare(query, [own_block])
            before = [(own_rows, own_keys, block) for block in range(step + 1)]
            before += [(far_rows, far_keys, block) for block in range(step)]
            compare(step, before)
        if step == 0:
            code_hop.wait_recv()
            spread(far_codes, far_keys, False)
        hop.wait_recv()
        if step < STRAIGHT:

            def others(query, _, far_block=far_block):
                compare(query, [far_block])
                return 0

            lax.fori_loop(0, step + 1, others, 0)
            continue
        for query in range(step + 1):
            compare(query, [far_block])
            if step < GROUPS - 1:
                continue
            for half in range(2):
                top = jnp.max(best[query, :, half * 128 : (half + 1) * 128], axis=0, keepdims=True)
                send_back[query * 2 + half] = top
            for index in range(query * GROUP, (query + 1) * GROUP):
                if index == 0:
                    got_back[0] = send_back[0]
                    continue
                copy = pltpu.make_async_remote_copy(
                    src_ref=send_back.at[index // 4], dst_ref=got_back.at[index],
                    send_sem=back_send, recv_sem=back_recv,
                    device_id=peer(ORDER[index], -1), device_id_type=MESH,
                )
                copy.start()

    pltpu.make_async_copy(got_back.at[1:], got_back.at[1:], back_recv).wait()
    back = got_back[...].reshape(OWNERS, 128)
    first = back.astype(jnp.bfloat16)
    rest = back - first.astype(jnp.float32)
    second = rest.astype(jnp.bfloat16)
    third = (rest - second.astype(jnp.float32)).astype(jnp.bfloat16)
    moved = [
        jnp.dot(piece, picks[...], preferred_element_type=jnp.float32)
        for piece in (first, second, third)
    ]
    moved = moved[0] + moved[1] + moved[2]
    result = jnp.sum(jnp.where(place[...] > 0.5, moved, 0.0), axis=0, keepdims=True)
    for tile in range(8):
        out_ref[tile : tile + 1, :] = result[:, tile * 128 : (tile + 1) * 128]

    pltpu.make_async_copy(send_rows.at[1:], send_rows.at[1:], row_send).wait()
    pltpu.make_async_copy(send_codes.at[1:], send_codes.at[1:], code_send).wait()
    pltpu.make_async_copy(got_back.at[1:], got_back.at[1:], back_send).wait()
    code_hop.wait_send()
    for hop in hops:
        hop.wait_send()


def shards(embeddings, cluster, rank):
    rows = (OWNERS, CAP, D)
    codes = (OWNERS, 1, 128)
    f32, bf16 = jnp.float32, jnp.bfloat16
    dma = pltpu.SemaphoreType.DMA
    result = pl.pallas_call(
        kernel,
        out_shape=jax.ShapeDtypeStruct((8, 128), f32),
        in_specs=[pl.BlockSpec(memory_space=pltpu.HBM)] * 3,
        out_specs=pl.BlockSpec(memory_space=pltpu.VMEM),
        scratch_shapes=[
            pltpu.VMEM((ROWS, D), bf16),
            pltpu.VMEM((8, 128), jnp.int32),
            pltpu.VMEM((8, 128), jnp.int32),
            pltpu.VMEM((ROWS, D), bf16),
            pltpu.VMEM((OWNERS, ROWS), bf16),
            pltpu.VMEM((OWNERS, ROWS), f32),
            pltpu.VMEM((WIDE, ROWS), bf16),
            pltpu.VMEM((128, ROWS), bf16),
            pltpu.VMEM(rows, bf16),
            pltpu.VMEM(rows, bf16),
            pltpu.VMEM(rows, bf16),
            pltpu.VMEM(codes, f32),
            pltpu.VMEM(codes, f32),
            pltpu.VMEM(codes, f32),
            pltpu.VMEM((OWNERS * CAP, 128), f32),
            pltpu.VMEM((OWNERS * CAP, 128), f32),
            pltpu.VMEM((2, OWNERS // 4, 1, 128), f32),
            pltpu.VMEM((GROUPS, 8, WIDE), f32),
            pltpu.VMEM((OWNERS // 4, 1, 128), f32),
            pltpu.VMEM(codes, f32),
            dma((3,)),
            dma,
            dma((GROUPS,)),
            dma,
            dma,
            dma((GROUPS + 1,)),
            dma((GROUPS + 1,)),
            dma,
            dma,
        ],
        compiler_params=pltpu.CompilerParams(
            collective_id=0, has_side_effects=True, vmem_limit_bytes=63 * 2**20
        ),
        cost_estimate=pl.CostEstimate(
            flops=2 * D * 2048 * (4096 + 1024), bytes_accessed=2 * ROWS * D, transcendentals=ROWS
        ),
        name="dedup",
    )(embeddings, cluster.reshape(8, 128), rank.reshape(8, 128))
    return result.reshape(ROWS)


def solution(mesh):
    in_specs = (P(("dp", "split"), None), P(("dp", "split")), P(("dp", "split")))
    out_specs = P(("dp", "split"))
    return jax.shard_map(shards, mesh=mesh, in_specs=in_specs, out_specs=out_specs, check_vma=False)
```

```python
import functools

import jax
import jax.numpy as jnp
from jax import lax
from jax.experimental import pallas as pl
from jax.experimental.pallas import tpu as pltpu
from jax.sharding import PartitionSpec as P

MESH = pl.DeviceIdType.MESH
OWNERS = 64
CAP = 32
ROWS = 1024
D = 768
RANKS = 131072
GROUP = 8
GROUPS = OWNERS // GROUP
WIDE = GROUP * CAP
EMPTY = 16777216.0


PLAN = (
    (25, 5, 11, 96),
    (8, 48, 144, 13, 37),
    (111, 166, 91, 77, 83),
    (124, 140, 87, 183),
    (116, 60, 150, 16, 136),
    (108, 31, 161, 47),
    (163, 142, 53, 23, 69, 147),
    (92, 126, 76),
    (81, 165, 112, 184, 125, 131),
    (175, 152, 138),
    (17, 191, 114, 61, 46),
    (51, 162, 79, 32),
    (109, 88, 149, 143, 75, 159),
    (128, 123, 82),
    (90, 174, 22, 139, 113, 167),
    (130, 44, 135),
    (185, 71, 78, 189, 115, 187),
    (141, 172, 164),
    (160, 40, 89, 119, 66, 153),
    (176, 99, 127),
    (129, 19, 43, 137, 95),
    (178, 80, 63, 186),
    (173, 59, 72, 168, 70, 190),
    (117, 34, 68),
    (157, 85, 41, 155, 102),
    (20, 93, 180, 28),
    (54, 177, 64, 133, 188),
    (169, 101, 107, 120),
    (35, 57, 171, 73),
    (84, 156, 67, 104),
    (118, 94, 29),
    (65, 179, 132, 181),
    (105, 121, 56),
)
WAIT = 5
LAND = 4
CODES_AT = 2
CODES_LAND = 8
HOP = 2
PAIRS = 6
LAST_PAIRS = 32


def step_of(code):
    return (code // 16, code // 4 % 4, code % 4)


def travel():
    hops, done, order = [], {}, [0]
    for entries in PLAN:
        row = []
        for entry in entries:
            code, dim = entry // 3, entry % 3
            passed = done.setdefault(code, set())
            first = not passed
            passed.add(dim)
            last = passed == {axis for axis, part in enumerate(step_of(code)) if part}
            if last:
                order.append(code)
            row.append((code, dim, first, last))
        hops.append(row)
    return hops, order


HOPS, ARRIVALS = travel()
ORDER = [step_of(code) for code in ARRIVALS]
SLOT = {code: slot for slot, code in enumerate(ARRIVALS)}
TRANSITS = sum(not last for row in HOPS for _, _, _, last in row)


def nt_dot(a, b):
    return lax.dot_general(a, b, (((1,), (1,)), ((), ())), preferred_element_type=jnp.float32)


def kernel(
    emb_hbm, cluster_hbm, rank_hbm, out_ref,
    emb, cluster, rank, unit, hits, place, sel, picks,
    send_rows, transit, own_rows, far_rows, send_codes, own_codes, far_codes,
    own_keys, far_keys, limits, best, send_back, got_back,
    load_sem, row_send, pass_send, pass_recv, row_recv, code_send, code_recv, far_send, far_recv, back_send, back_recv,
):
    me = lax.axis_index("dp")
    core = lax.axis_index("split")
    my, mz, mx = me // 16, me // 4 % 4, me % 4

    def peer(step, sign):
        y = (my + sign * step[0] + 4) % 4
        z = (mz + sign * step[1] + 4) % 4
        x = (mx + sign * step[2] + 4) % 4
        return (y * 16 + z * 4 + x, core)

    sibling = (me, 1 - core)

    loads = [
        pltpu.make_async_copy(source, target, load_sem.at[index])
        for index, (source, target) in enumerate(
            ((cluster_hbm, cluster), (rank_hbm, rank), (emb_hbm, emb))
        )
    ]
    for load in loads:
        load.start()
    barrier = pltpu.get_barrier_semaphore()
    for step in ORDER[1:]:
        pl.semaphore_signal(barrier, inc=1, device_id=peer(step, 1), device_id_type=MESH)
    pl.semaphore_signal(barrier, inc=1, device_id=sibling, device_id_type=MESH)

    loads[0].wait()
    loads[1].wait()
    slot = lax.broadcasted_iota(jnp.int32, (OWNERS, 128), 0)
    route = jnp.zeros((OWNERS, 128), jnp.int32)
    for index, step in enumerate(ORDER):
        route = jnp.where(slot == index, step[0] * 16 + step[1] * 4 + step[2], route)
    words = []
    for tile in range(8):
        ids = cluster[tile : tile + 1, :]
        owner = ids // 8
        step_y = (owner // 16 - my + 4) % 4
        step_z = (owner // 4 % 4 - mz + 4) % 4
        step_x = (owner % 4 - mx + 4) % 4
        code = step_y * 16 + step_z * 4 + step_x
        hit = jnp.where(route == code, 1.0, 0.0)
        hits[:, tile * 128 : (tile + 1) * 128] = hit.astype(jnp.bfloat16)
        words.append(ids % 8 * RANKS + rank[tile : tile + 1, :] + 1)
    lower = lax.broadcasted_iota(jnp.int32, (256, 256), 0)
    upper = lax.broadcasted_iota(jnp.int32, (256, 256), 1)
    before = jnp.where(lower <= upper, 1.0, 0.0).astype(jnp.bfloat16)
    carry = jnp.zeros((OWNERS, 1), jnp.float32)
    for part in range(4):
        cols = slice(part * 256, (part + 1) * 256)
        count = jnp.dot(hits[:, cols], before, preferred_element_type=jnp.float32) + carry
        carry = count[:, 255:256]
        place[:, cols] = jnp.where(hits[:, cols].astype(jnp.float32) > 0.5, count, 0.0)
    loads[2].wait()

    def normalise(index, _):
        rows = pl.ds(pl.multiple_of(index * 128, 128), 128)
        values = emb[rows, :].astype(jnp.float32)
        total = jnp.sum(values * values, axis=1, keepdims=True)
        unit[rows, :] = (values * lax.rsqrt(total + 1e-06)).astype(jnp.bfloat16)
        return 0

    lax.fori_loop(0, 8, normalise, 0)

    leaving = [SLOT[code] for row in HOPS for code, _, first, _ in row if first]
    leaving.insert(GROUP * 2 - 1, 0)
    spot = lax.broadcasted_iota(jnp.int32, (CAP, ROWS), 0).astype(jnp.float32) + 1.0
    selected = []

    def select_until(count):
        while len(selected) < count:
            slots = leaving[len(selected) : len(selected) + GROUP]
            for index, slot in enumerate(slots):
                line = place[slot : slot + 1, :]
                chosen = jnp.where(jnp.broadcast_to(line, (CAP, ROWS)) == spot, 1.0, 0.0)
                sel[index * CAP : (index + 1) * CAP, :] = chosen.astype(jnp.bfloat16)
            picked = jnp.dot(sel[...], unit[...], preferred_element_type=jnp.float32)
            picked = picked.astype(jnp.bfloat16).reshape(GROUP, CAP, D)
            for index, slot in enumerate(slots):
                if slot == 0:
                    own_rows[0] = picked[index]
                else:
                    send_rows[slot] = picked[index]
            selected.extend(slots)

    def needed(number):
        slots = [SLOT[code] for row in HOPS[: number + 1] for code, _, first, _ in row if first]
        return max((leaving.index(slot) + 1 for slot in slots), default=0)

    def send_all_codes():
        turn = lax.broadcasted_iota(jnp.int32, (OWNERS, ROWS), 0) % 4 * CAP
        where = jnp.where(place[...] > 0.5, place[...] - 1.0 + turn.astype(jnp.float32), 0.0)
        where = jnp.sum(where, axis=0, keepdims=True)
        lane = lax.broadcasted_iota(jnp.int32, (128, ROWS), 0).astype(jnp.float32)
        picks[...] = jnp.where(lane == where, 1.0, 0.0).astype(jnp.bfloat16)

        word = jnp.concatenate(words, axis=1)
        codes = jnp.zeros((OWNERS, 128), jnp.float32)
        for power, digit in ((1, word % 256), (256, word // 256 % 256), (65536, word // 65536)):
            marked = hits[...] * digit.astype(jnp.float32).astype(jnp.bfloat16)
            codes = codes + nt_dot(marked, picks[...]) * float(power)
        send_codes[...] = codes.reshape(OWNERS, 1, 128)
        own_codes[0] = send_codes[0]
        for index in range(1, OWNERS):
            copy = pltpu.make_async_remote_copy(
                src_ref=send_codes.at[index], dst_ref=own_codes.at[index],
                send_sem=code_send, recv_sem=code_recv,
                device_id=peer(ORDER[index], 1), device_id_type=MESH,
            )
            copy.start()

    def spread(codes, keys, is_own):
        block = codes[...].reshape(OWNERS // 4, 4, 1, 128)
        line = jnp.sum(block, axis=1)
        if is_own:
            limits[0] = line
            limits[1] = jnp.floor((line - 1.0) * (1.0 / RANKS)) * float(RANKS) + 1.0
        line = jnp.where(line == 0.0, EMPTY, line)
        for index in range(OWNERS // 4):
            square = jnp.broadcast_to(line[index], (128, 128))
            keys[index * 128 : (index + 1) * 128, :] = square.T

    def compare(query, blocks):
        rows = own_rows[query * GROUP : (query + 1) * GROUP].reshape(WIDE, D)
        high = limits[0, query * 2 : query * 2 + 2]
        low = limits[1, query * 2 : query * 2 + 2]
        tops = [best[query, :, half * 128 : (half + 1) * 128] for half in range(2)]
        for is_far, block in blocks:
            data, keys = (far_rows, far_keys) if is_far else (own_rows, own_keys)
            scores = nt_dot(data[block * GROUP : (block + 1) * GROUP].reshape(WIDE, D), rows)
            code = keys[block * WIDE : (block + 1) * WIDE, :]
            for half in range(2):
                allowed = (code < high[half]) & (code >= low[half])
                part = scores[:, half * 128 : (half + 1) * 128]
                part = jnp.where(allowed, part, -1.0).reshape(WIDE // 8, 8, 128)
                tops[half] = jnp.maximum(tops[half], jnp.max(part, axis=0))
        for half in range(2):
            best[query, :, half * 128 : (half + 1) * 128] = tops[half]

    def finish():
        tops = jnp.max(best[...], axis=1)
        for query in range(GROUPS):
            for half in range(2):
                send_back[query * 2 + half] = tops[query : query + 1, half * 128 : (half + 1) * 128]
        got_back[0] = send_back[0]
        for index in range(1, OWNERS):
            copy = pltpu.make_async_remote_copy(
                src_ref=send_back.at[index // 4], dst_ref=got_back.at[index],
                send_sem=back_send, recv_sem=back_recv,
                device_id=peer(ORDER[index], -1), device_id_type=MESH,
            )
            copy.start()

    best[...] = jnp.full(best.shape, -1.0, jnp.float32)
    queries, blocks, pairs, hops = [], [], [], []

    def compare_some(count):
        now = pairs[:count]
        del pairs[:count]
        while now:
            query = now[0][0]
            together = [block for other, block in now if other == query]
            now = [pair for pair in now if pair[0] != query]
            compare(query, together)

    def exchange(source, target, index):
        hop = pltpu.make_async_remote_copy(
            src_ref=source, dst_ref=target,
            send_sem=far_send.at[index], recv_sem=far_recv.at[index],
            device_id=sibling, device_id_type=MESH,
        )
        hop.start()
        hops.append(hop)
        return hop

    def codes_here():
        pltpu.make_async_copy(own_codes.at[1:], own_codes.at[1:], code_recv).wait()
        hop = exchange(own_codes, far_codes, GROUPS)
        spread(own_codes, own_keys, True)
        return lambda: codes_there(hop)

    def codes_there(hop):
        hop.wait_recv()
        spread(far_codes, far_keys, False)

    def group_here(group):
        here = own_rows.at[max(1, group * GROUP) : (group + 1) * GROUP]
        pltpu.make_async_copy(here, here, row_recv.at[group]).wait()
        rows = pl.ds(group * GROUP, GROUP)
        hop = exchange(own_rows.at[rows], far_rows.at[rows], group)
        pairs.extend((query, (False, group)) for query in queries)
        queries.append(group)
        blocks.append((False, group))
        pairs.extend((group, block) for block in blocks)
        return lambda: group_there(group, hop)

    def group_there(group, hop):
        hop.wait_recv()
        if group == GROUPS - 1:
            compare_some(len(pairs))
            for query in queries:
                compare(query, [(True, group)])
            finish()
            return
        blocks.append((True, group))
        pairs.extend((query, (True, group)) for query in queries)

    events, arrived = {}, 0
    for number, row in enumerate(HOPS):
        arrived += sum(last for _, _, _, last in row)
        for group in range(GROUPS):
            if arrived >= group * GROUP + GROUP - 1 and group not in events:
                events[group] = number + LAND
    todo = [(CODES_LAND, codes_here)]
    todo += [(max(CODES_LAND, events[group]), functools.partial(group_here, group)) for group in range(GROUPS)]
    parked, pass_at, number = {}, 0, 0
    select_until(needed(CODES_AT - 1))
    pl.semaphore_wait(barrier, OWNERS)
    while number < len(HOPS) or todo or pairs:
        if number == CODES_AT:
            send_all_codes()
        if number < len(HOPS):
            if number >= WAIT and number - WAIT in parked:
                here = transit.at[parked[number - WAIT]]
                pltpu.make_async_copy(here, here, pass_recv.at[number - WAIT]).wait()
            start = pass_at
            for code, dim, first, last in HOPS[number]:
                slot = SLOT[code]
                target = [0, 0, 0]
                target[dim] = step_of(code)[dim]
                if last:
                    place_there, arrival = own_rows.at[slot], row_recv.at[slot // GROUP]
                else:
                    place_there, arrival = transit.at[pass_at], pass_recv.at[number]
                copy = pltpu.make_async_remote_copy(
                    src_ref=send_rows.at[slot] if first else transit.at[parked[code, "at"]],
                    dst_ref=place_there,
                    send_sem=row_send if first else pass_send,
                    recv_sem=arrival,
                    device_id=peer(target, 1), device_id_type=MESH,
                )
                copy.start()
                if not last:
                    parked[code, "at"] = pass_at
                    pass_at += 1
            if pass_at > start:
                parked[number] = pl.ds(start, pass_at - start)
            select_until(needed(number + 2))
        for event in [event for event in todo if event[0] <= number]:
            todo.remove(event)
            following = event[1]()
            if following:
                todo.append((number + HOP, following))
        compare_some(PAIRS if number < len(HOPS) else LAST_PAIRS)
        number += 1

    pltpu.make_async_copy(got_back.at[1:], got_back.at[1:], back_recv).wait()
    back = got_back[...].reshape(OWNERS, 128)
    first = back.astype(jnp.bfloat16)
    rest = back - first.astype(jnp.float32)
    second = rest.astype(jnp.bfloat16)
    third = (rest - second.astype(jnp.float32)).astype(jnp.bfloat16)
    moved = [
        jnp.dot(piece, picks[...], preferred_element_type=jnp.float32)
        for piece in (first, second, third)
    ]
    moved = moved[0] + moved[1] + moved[2]
    result = jnp.sum(jnp.where(place[...] > 0.5, moved, 0.0), axis=0, keepdims=True)
    for tile in range(8):
        out_ref[tile : tile + 1, :] = result[:, tile * 128 : (tile + 1) * 128]

    pltpu.make_async_copy(send_rows.at[1:], send_rows.at[1:], row_send).wait()
    pltpu.make_async_copy(transit, transit, pass_send).wait()
    pltpu.make_async_copy(send_codes.at[1:], send_codes.at[1:], code_send).wait()
    pltpu.make_async_copy(got_back.at[1:], got_back.at[1:], back_send).wait()
    for hop in hops:
        hop.wait_send()


def shards(embeddings, cluster, rank):
    rows = (OWNERS, CAP, D)
    codes = (OWNERS, 1, 128)
    f32, bf16 = jnp.float32, jnp.bfloat16
    dma = pltpu.SemaphoreType.DMA
    result = pl.pallas_call(
        kernel,
        out_shape=jax.ShapeDtypeStruct((8, 128), f32),
        in_specs=[pl.BlockSpec(memory_space=pltpu.HBM)] * 3,
        out_specs=pl.BlockSpec(memory_space=pltpu.VMEM),
        scratch_shapes=[
            pltpu.VMEM((ROWS, D), bf16),
            pltpu.VMEM((8, 128), jnp.int32),
            pltpu.VMEM((8, 128), jnp.int32),
            pltpu.VMEM((ROWS, D), bf16),
            pltpu.VMEM((OWNERS, ROWS), bf16),
            pltpu.VMEM((OWNERS, ROWS), f32),
            pltpu.VMEM((WIDE, ROWS), bf16),
            pltpu.VMEM((128, ROWS), bf16),
            pltpu.VMEM(rows, bf16),
            pltpu.VMEM((TRANSITS, CAP, D), bf16),
            pltpu.VMEM(rows, bf16),
            pltpu.VMEM(rows, bf16),
            pltpu.VMEM(codes, f32),
            pltpu.VMEM(codes, f32),
            pltpu.VMEM(codes, f32),
            pltpu.VMEM((OWNERS * CAP, 128), f32),
            pltpu.VMEM((OWNERS * CAP, 128), f32),
            pltpu.VMEM((2, OWNERS // 4, 1, 128), f32),
            pltpu.VMEM((GROUPS, 8, WIDE), f32),
            pltpu.VMEM((OWNERS // 4, 1, 128), f32),
            pltpu.VMEM(codes, f32),
            dma((3,)),
            dma,
            dma,
            dma((len(HOPS),)),
            dma((GROUPS,)),
            dma,
            dma,
            dma((GROUPS + 1,)),
            dma((GROUPS + 1,)),
            dma,
            dma,
        ],
        compiler_params=pltpu.CompilerParams(
            collective_id=0, has_side_effects=True, vmem_limit_bytes=63 * 2**20
        ),
        cost_estimate=pl.CostEstimate(
            flops=2 * D * 2048 * (4096 + 1024), bytes_accessed=2 * ROWS * D, transcendentals=ROWS
        ),
        name="dedup",
    )(embeddings, cluster.reshape(8, 128), rank.reshape(8, 128))
    return result.reshape(ROWS)


def solution(mesh):
    in_specs = (P(("dp", "split"), None), P(("dp", "split")), P(("dp", "split")))
    out_specs = P(("dp", "split"))
    return jax.shard_map(shards, mesh=mesh, in_specs=in_specs, out_specs=out_specs, check_vma=False)
```

```python
import functools

import jax
import jax.numpy as jnp
from jax import lax
from jax.experimental import pallas as pl
from jax.experimental.pallas import tpu as pltpu
from jax.sharding import PartitionSpec as P

MESH = pl.DeviceIdType.MESH
OWNERS = 64
CAP = 32
ROWS = 1024
D = 768
RANKS = 131072
GROUP = 8
GROUPS = OWNERS // GROUP
WIDE = GROUP * CAP
EMPTY = 16777216.0


PLAN = (
    (25, 5, 11, 96),
    (8, 48, 144, 13, 37),
    (111, 166, 91, 77, 83),
    (124, 140, 87, 183),
    (116, 60, 150, 16, 136),
    (108, 31, 161, 47),
    (163, 142, 53, 23, 69, 147),
    (92, 126, 76),
    (81, 165, 112, 184, 125, 131),
    (175, 152, 138),
    (17, 191, 114, 61, 46),
    (51, 162, 79, 32),
    (109, 88, 149, 143, 75, 159),
    (128, 123, 82),
    (90, 174, 22, 139, 113, 167),
    (130, 44, 135),
    (185, 71, 78, 189, 115, 187),
    (141, 172, 164),
    (160, 40, 89, 119, 66, 153),
    (176, 99, 127),
    (129, 19, 43, 137, 95),
    (178, 80, 63, 186),
    (173, 59, 72, 168, 70, 190),
    (117, 34, 68),
    (157, 85, 41, 155, 102),
    (20, 93, 180, 28),
    (54, 177, 64, 133, 188),
    (169, 101, 107, 120),
    (35, 57, 171, 73),
    (84, 156, 67, 104),
    (118, 94, 29),
    (65, 179, 132, 181),
    (105, 121, 56),
)
WAIT = 5
LAND = 5
CODES_AT = 2
CODES_LAND = 8
HOP = 2
PAIRS = 7
LAST_PAIRS = 32


def step_of(code):
    return (code // 16, code // 4 % 4, code % 4)


def hops_of(step):
    return sum(min(part, 4 - part) for part in step)


def travel():
    hops, done, order = [], {}, [0]
    for entries in PLAN:
        row = []
        for entry in entries:
            code, dim = entry // 3, entry % 3
            passed = done.setdefault(code, set())
            first = not passed
            passed.add(dim)
            last = passed == {axis for axis, part in enumerate(step_of(code)) if part}
            if last:
                order.append(code)
            row.append((code, dim, first, last))
        hops.append(row)
    return hops, order


HOPS, ARRIVALS = travel()
ORDER = [step_of(code) for code in ARRIVALS]
SLOT = {code: slot for slot, code in enumerate(ARRIVALS)}
TRANSITS = sum(not last for row in HOPS for _, _, _, last in row)


def nt_dot(a, b):
    return lax.dot_general(a, b, (((1,), (1,)), ((), ())), preferred_element_type=jnp.float32)


def kernel(
    emb_hbm, cluster_hbm, rank_hbm, out_ref,
    emb, cluster, rank, unit, hits, place, sel, picks,
    send_rows, transit, own_rows, far_rows, send_codes, own_codes, far_codes,
    own_keys, far_keys, limits, best, send_back, got_back,
    load_sem, row_send, pass_send, pass_recv, row_recv, code_send, code_recv, far_send, far_recv, back_send, back_recv,
):
    me = lax.axis_index("dp")
    core = lax.axis_index("split")
    my, mz, mx = me // 16, me // 4 % 4, me % 4

    def peer(step, sign):
        y = (my + sign * step[0] + 4) % 4
        z = (mz + sign * step[1] + 4) % 4
        x = (mx + sign * step[2] + 4) % 4
        return (y * 16 + z * 4 + x, core)

    sibling = (me, 1 - core)

    loads = [
        pltpu.make_async_copy(source, target, load_sem.at[index])
        for index, (source, target) in enumerate(
            ((cluster_hbm, cluster), (rank_hbm, rank), (emb_hbm, emb))
        )
    ]
    for load in loads:
        load.start()
    barrier = pltpu.get_barrier_semaphore()
    for step in ORDER[1:]:
        pl.semaphore_signal(barrier, inc=1, device_id=peer(step, 1), device_id_type=MESH)
    pl.semaphore_signal(barrier, inc=1, device_id=sibling, device_id_type=MESH)

    loads[0].wait()
    loads[1].wait()
    slot = lax.broadcasted_iota(jnp.int32, (OWNERS, 128), 0)
    route = jnp.zeros((OWNERS, 128), jnp.int32)
    for index, step in enumerate(ORDER):
        route = jnp.where(slot == index, step[0] * 16 + step[1] * 4 + step[2], route)
    words = []
    for tile in range(8):
        ids = cluster[tile : tile + 1, :]
        owner = ids // 8
        step_y = (owner // 16 - my + 4) % 4
        step_z = (owner // 4 % 4 - mz + 4) % 4
        step_x = (owner % 4 - mx + 4) % 4
        code = step_y * 16 + step_z * 4 + step_x
        hit = jnp.where(route == code, 1.0, 0.0)
        hits[:, tile * 128 : (tile + 1) * 128] = hit.astype(jnp.bfloat16)
        words.append(ids % 8 * RANKS + rank[tile : tile + 1, :] + 1)
    lower = lax.broadcasted_iota(jnp.int32, (256, 256), 0)
    upper = lax.broadcasted_iota(jnp.int32, (256, 256), 1)
    before = jnp.where(lower <= upper, 1.0, 0.0).astype(jnp.bfloat16)
    carry = jnp.zeros((OWNERS, 1), jnp.float32)
    for part in range(4):
        cols = slice(part * 256, (part + 1) * 256)
        count = jnp.dot(hits[:, cols], before, preferred_element_type=jnp.float32) + carry
        carry = count[:, 255:256]
        place[:, cols] = jnp.where(hits[:, cols].astype(jnp.float32) > 0.5, count, 0.0)
    loads[2].wait()

    def normalise(index, _):
        rows = pl.ds(pl.multiple_of(index * 128, 128), 128)
        values = emb[rows, :].astype(jnp.float32)
        total = jnp.sum(values * values, axis=1, keepdims=True)
        unit[rows, :] = (values * lax.rsqrt(total + 1e-06)).astype(jnp.bfloat16)
        return 0

    lax.fori_loop(0, 8, normalise, 0)

    leaving = [SLOT[code] for row in HOPS for code, _, first, _ in row if first]
    leaving.insert(GROUP * 2 - 1, 0)
    spot = lax.broadcasted_iota(jnp.int32, (CAP, ROWS), 0).astype(jnp.float32) + 1.0
    selected = []

    def select_until(count):
        while len(selected) < count:
            slots = leaving[len(selected) : len(selected) + GROUP]
            for index, slot in enumerate(slots):
                line = place[slot : slot + 1, :]
                chosen = jnp.where(jnp.broadcast_to(line, (CAP, ROWS)) == spot, 1.0, 0.0)
                sel[index * CAP : (index + 1) * CAP, :] = chosen.astype(jnp.bfloat16)
            picked = jnp.dot(sel[...], unit[...], preferred_element_type=jnp.float32)
            picked = picked.astype(jnp.bfloat16).reshape(GROUP, CAP, D)
            for index, slot in enumerate(slots):
                if slot == 0:
                    own_rows[0] = picked[index]
                else:
                    send_rows[slot] = picked[index]
            selected.extend(slots)

    def needed(number):
        slots = [SLOT[code] for row in HOPS[: number + 1] for code, _, first, _ in row if first]
        return max((leaving.index(slot) + 1 for slot in slots), default=0)

    def send_all_codes():
        turn = lax.broadcasted_iota(jnp.int32, (OWNERS, ROWS), 0) % 4 * CAP
        where = jnp.where(place[...] > 0.5, place[...] - 1.0 + turn.astype(jnp.float32), 0.0)
        where = jnp.sum(where, axis=0, keepdims=True)
        lane = lax.broadcasted_iota(jnp.int32, (128, ROWS), 0).astype(jnp.float32)
        picks[...] = jnp.where(lane == where, 1.0, 0.0).astype(jnp.bfloat16)

        word = jnp.concatenate(words, axis=1)
        codes = jnp.zeros((OWNERS, 128), jnp.float32)
        for power, digit in ((1, word % 256), (256, word // 256 % 256), (65536, word // 65536)):
            marked = hits[...] * digit.astype(jnp.float32).astype(jnp.bfloat16)
            codes = codes + nt_dot(marked, picks[...]) * float(power)
        send_codes[...] = codes.reshape(OWNERS, 1, 128)
        own_codes[0] = send_codes[0]
        for index in range(1, OWNERS):
            copy = pltpu.make_async_remote_copy(
                src_ref=send_codes.at[index], dst_ref=own_codes.at[index],
                send_sem=code_send, recv_sem=code_recv,
                device_id=peer(ORDER[index], 1), device_id_type=MESH,
            )
            copy.start()

    def spread(codes, keys, is_own):
        block = codes[...].reshape(OWNERS // 4, 4, 1, 128)
        line = jnp.sum(block, axis=1)
        if is_own:
            limits[0] = line
            limits[1] = jnp.floor((line - 1.0) * (1.0 / RANKS)) * float(RANKS) + 1.0
        line = jnp.where(line == 0.0, EMPTY, line)
        for index in range(OWNERS // 4):
            square = jnp.broadcast_to(line[index], (128, 128))
            keys[index * 128 : (index + 1) * 128, :] = square.T

    def compare(query, blocks):
        rows = own_rows[query * GROUP : (query + 1) * GROUP].reshape(WIDE, D)
        high = limits[0, query * 2 : query * 2 + 2]
        low = limits[1, query * 2 : query * 2 + 2]
        tops = [best[query, :, half * 128 : (half + 1) * 128] for half in range(2)]
        for is_far, block in blocks:
            data, keys = (far_rows, far_keys) if is_far else (own_rows, own_keys)
            scores = nt_dot(data[block * GROUP : (block + 1) * GROUP].reshape(WIDE, D), rows)
            code = keys[block * WIDE : (block + 1) * WIDE, :]
            for half in range(2):
                allowed = (code < high[half]) & (code >= low[half])
                part = scores[:, half * 128 : (half + 1) * 128]
                part = jnp.where(allowed, part, -1.0).reshape(WIDE // 8, 8, 128)
                tops[half] = jnp.maximum(tops[half], jnp.max(part, axis=0))
        for half in range(2):
            best[query, :, half * 128 : (half + 1) * 128] = tops[half]

    def finish():
        tops = jnp.max(best[...], axis=1)
        for query in range(GROUPS):
            for half in range(2):
                send_back[query * 2 + half] = tops[query : query + 1, half * 128 : (half + 1) * 128]
        got_back[0] = send_back[0]
        for index in sorted(range(1, OWNERS), key=lambda index: -hops_of(ORDER[index])):
            copy = pltpu.make_async_remote_copy(
                src_ref=send_back.at[index // 4], dst_ref=got_back.at[index],
                send_sem=back_send, recv_sem=back_recv,
                device_id=peer(ORDER[index], -1), device_id_type=MESH,
            )
            copy.start()

    best[...] = jnp.full(best.shape, -1.0, jnp.float32)
    queries, blocks, pairs, hops = [], [], [], []

    def compare_some(count):
        now = pairs[:count]
        del pairs[:count]
        while now:
            query = now[0][0]
            together = [block for other, block in now if other == query]
            now = [pair for pair in now if pair[0] != query]
            compare(query, together)

    def exchange(source, target, index):
        hop = pltpu.make_async_remote_copy(
            src_ref=source, dst_ref=target,
            send_sem=far_send.at[index], recv_sem=far_recv.at[index],
            device_id=sibling, device_id_type=MESH,
        )
        hop.start()
        hops.append(hop)
        return hop

    def codes_here():
        pltpu.make_async_copy(own_codes.at[1:], own_codes.at[1:], code_recv).wait()
        hop = exchange(own_codes, far_codes, GROUPS)
        spread(own_codes, own_keys, True)
        return lambda: codes_there(hop)

    def codes_there(hop):
        hop.wait_recv()
        spread(far_codes, far_keys, False)

    def group_here(group):
        here = own_rows.at[max(1, group * GROUP) : (group + 1) * GROUP]
        pltpu.make_async_copy(here, here, row_recv.at[group]).wait()
        rows = pl.ds(group * GROUP, GROUP)
        hop = exchange(own_rows.at[rows], far_rows.at[rows], group)
        pairs.extend((query, (False, group)) for query in queries)
        queries.append(group)
        blocks.append((False, group))
        pairs.extend((group, block) for block in blocks)
        return lambda: group_there(group, hop)

    def group_there(group, hop):
        hop.wait_recv()
        if group == GROUPS - 1:
            compare_some(len(pairs))
            for query in queries:
                compare(query, [(True, group)])
            finish()
            return
        blocks.append((True, group))
        pairs.extend((query, (True, group)) for query in queries)

    events, arrived = {}, 0
    for number, row in enumerate(HOPS):
        arrived += sum(last for _, _, _, last in row)
        for group in range(GROUPS):
            if arrived >= group * GROUP + GROUP - 1 and group not in events:
                events[group] = number + LAND
    todo = [(CODES_LAND, codes_here)]
    todo += [(max(CODES_LAND, events[group]), functools.partial(group_here, group)) for group in range(GROUPS)]
    parked, pass_at, number = {}, 0, 0
    select_until(needed(CODES_AT - 1))
    pl.semaphore_wait(barrier, OWNERS)
    while number < len(HOPS) or todo or pairs:
        if number == CODES_AT:
            send_all_codes()
        if number < len(HOPS):
            if number >= WAIT and number - WAIT in parked:
                here = transit.at[parked[number - WAIT]]
                pltpu.make_async_copy(here, here, pass_recv.at[number - WAIT]).wait()
            start = pass_at
            for code, dim, first, last in HOPS[number]:
                slot = SLOT[code]
                target = [0, 0, 0]
                target[dim] = step_of(code)[dim]
                if last:
                    place_there, arrival = own_rows.at[slot], row_recv.at[slot // GROUP]
                else:
                    place_there, arrival = transit.at[pass_at], pass_recv.at[number]
                copy = pltpu.make_async_remote_copy(
                    src_ref=send_rows.at[slot] if first else transit.at[parked[code, "at"]],
                    dst_ref=place_there,
                    send_sem=row_send if first else pass_send,
                    recv_sem=arrival,
                    device_id=peer(target, 1), device_id_type=MESH,
                )
                copy.start()
                if not last:
                    parked[code, "at"] = pass_at
                    pass_at += 1
            if pass_at > start:
                parked[number] = pl.ds(start, pass_at - start)
            select_until(needed(number + 2))
        for event in [event for event in todo if event[0] <= number]:
            todo.remove(event)
            following = event[1]()
            if following:
                todo.append((number + HOP, following))
        compare_some(PAIRS if number < len(HOPS) else LAST_PAIRS)
        number += 1

    pltpu.make_async_copy(got_back.at[1:], got_back.at[1:], back_recv).wait()
    back = got_back[...].reshape(OWNERS, 128)
    first = back.astype(jnp.bfloat16)
    rest = back - first.astype(jnp.float32)
    second = rest.astype(jnp.bfloat16)
    third = (rest - second.astype(jnp.float32)).astype(jnp.bfloat16)
    moved = jnp.dot(
        jnp.concatenate([first, second, third], axis=0), picks[...], preferred_element_type=jnp.float32
    )
    moved = moved[:OWNERS] + moved[OWNERS : 2 * OWNERS] + moved[2 * OWNERS :]
    result = jnp.sum(jnp.where(place[...] > 0.5, moved, 0.0), axis=0, keepdims=True)
    for tile in range(8):
        out_ref[tile : tile + 1, :] = result[:, tile * 128 : (tile + 1) * 128]

    pltpu.make_async_copy(send_rows.at[1:], send_rows.at[1:], row_send).wait()
    pltpu.make_async_copy(transit, transit, pass_send).wait()
    pltpu.make_async_copy(send_codes.at[1:], send_codes.at[1:], code_send).wait()
    pltpu.make_async_copy(got_back.at[1:], got_back.at[1:], back_send).wait()
    for hop in hops:
        hop.wait_send()


def shards(embeddings, cluster, rank):
    rows = (OWNERS, CAP, D)
    codes = (OWNERS, 1, 128)
    f32, bf16 = jnp.float32, jnp.bfloat16
    operands = (embeddings, cluster.reshape(8, 128), rank.reshape(8, 128))
    dma = pltpu.SemaphoreType.DMA
    result = pl.pallas_call(
        kernel,
        out_shape=jax.ShapeDtypeStruct((8, 128), f32),
        in_specs=[pl.BlockSpec(memory_space=pltpu.HBM)] * 3,
        out_specs=pl.BlockSpec(memory_space=pltpu.VMEM),
        scratch_shapes=[
            pltpu.VMEM((ROWS, D), bf16),
            pltpu.VMEM((8, 128), jnp.int32),
            pltpu.VMEM((8, 128), jnp.int32),
            pltpu.VMEM((ROWS, D), bf16),
            pltpu.VMEM((OWNERS, ROWS), bf16),
            pltpu.VMEM((OWNERS, ROWS), f32),
            pltpu.VMEM((WIDE, ROWS), bf16),
            pltpu.VMEM((128, ROWS), bf16),
            pltpu.VMEM(rows, bf16),
            pltpu.VMEM((TRANSITS, CAP, D), bf16),
            pltpu.VMEM(rows, bf16),
            pltpu.VMEM(rows, bf16),
            pltpu.VMEM(codes, f32),
            pltpu.VMEM(codes, f32),
            pltpu.VMEM(codes, f32),
            pltpu.VMEM((OWNERS * CAP, 128), f32),
            pltpu.VMEM((OWNERS * CAP, 128), f32),
            pltpu.VMEM((2, OWNERS // 4, 1, 128), f32),
            pltpu.VMEM((GROUPS, 8, WIDE), f32),
            pltpu.VMEM((OWNERS // 4, 1, 128), f32),
            pltpu.VMEM(codes, f32),
            dma((3,)),
            dma,
            dma,
            dma((len(HOPS),)),
            dma((GROUPS,)),
            dma,
            dma,
            dma((GROUPS + 1,)),
            dma((GROUPS + 1,)),
            dma,
            dma,
        ],
        compiler_params=pltpu.CompilerParams(
            collective_id=0, has_side_effects=True, vmem_limit_bytes=48 * 2**20
        ),
        cost_estimate=pl.CostEstimate(
            flops=2 * D * 2048 * (4096 + 1024), bytes_accessed=2 * ROWS * D, transcendentals=ROWS
        ),
        name="dedup",
    )(*(pltpu.with_memory_space_constraint(operand, pltpu.HBM) for operand in operands))
    return result.reshape(ROWS)


def solution(mesh):
    in_specs = (P(("dp", "split"), None), P(("dp", "split")), P(("dp", "split")))
    out_specs = P(("dp", "split"))
    return jax.shard_map(shards, mesh=mesh, in_specs=in_specs, out_specs=out_specs, check_vma=False)
```

```python
import functools

import jax
import jax.numpy as jnp
from jax import lax
from jax.experimental import pallas as pl
from jax.experimental.pallas import tpu as pltpu
from jax.sharding import PartitionSpec as P

MESH = pl.DeviceIdType.MESH
OWNERS = 64
CAP = 32
ROWS = 1024
D = 768
RANKS = 131072
GROUP = 8
GROUPS = OWNERS // GROUP
WIDE = GROUP * CAP
EMPTY = 16777216.0


PLAN = (
    (25, 5, 11, 96),
    (8, 48, 144, 13, 37),
    (111, 166, 91, 77, 83),
    (124, 140, 87, 183),
    (116, 60, 150, 16, 136),
    (108, 31, 161, 47),
    (163, 142, 53, 23, 69, 147),
    (92, 126, 76),
    (81, 165, 112, 184, 125, 131),
    (175, 152, 138),
    (17, 191, 114, 61, 46),
    (51, 162, 79, 32),
    (109, 88, 149, 143, 75, 159),
    (128, 123, 82),
    (90, 174, 22, 139, 113, 167),
    (130, 44, 135),
    (185, 71, 78, 189, 115, 187),
    (141, 172, 164),
    (160, 40, 89, 119, 66, 153),
    (176, 99, 127),
    (129, 19, 43, 137, 95),
    (178, 80, 63, 186),
    (173, 59, 72, 168, 70, 190),
    (117, 34, 68),
    (157, 85, 41, 155, 102),
    (20, 93, 180, 28),
    (54, 177, 64, 133, 188),
    (169, 101, 107, 120),
    (35, 57, 171, 73),
    (84, 156, 67, 104),
    (118, 94, 29),
    (65, 179, 132, 181),
    (105, 121, 56),
)
WAIT = 5
LAND = 5
PLANE_AT = 2
CODES_AT = 4
CODES_LAND = 9
HOP = 2
PAIRS = 7
LAST_PAIRS = 32


def step_of(code):
    return (code // 16, code // 4 % 4, code % 4)


def hops_of(step):
    return sum(min(part, 4 - part) for part in step)


def travel():
    hops, done, order = [], {}, [0]
    for entries in PLAN:
        row = []
        for entry in entries:
            code, dim = entry // 3, entry % 3
            passed = done.setdefault(code, set())
            first = not passed
            passed.add(dim)
            last = passed == {axis for axis, part in enumerate(step_of(code)) if part}
            if last:
                order.append(code)
            row.append((code, dim, first, last))
        hops.append(row)
    return hops, order


HOPS, ARRIVALS = travel()
ORDER = [step_of(code) for code in ARRIVALS]
SLOT = {code: slot for slot, code in enumerate(ARRIVALS)}
TRANSITS = sum(not last for row in HOPS for _, _, _, last in row)


def nt_dot(a, b):
    return lax.dot_general(a, b, (((1,), (1,)), ((), ())), preferred_element_type=jnp.float32)


def kernel(
    emb_hbm, cluster_hbm, rank_hbm, out_ref,
    emb, cluster, rank, unit, hits, place, sel, picks,
    send_rows, transit, own_rows, far_rows, send_codes, own_codes, far_codes,
    own_keys, far_keys, limits, best, send_back, got_back,
    load_sem, row_send, pass_send, pass_recv, row_recv, code_send, code_recv, far_send, far_recv, back_send, back_recv,
    plane_sem, cube_sem,
):
    me = lax.axis_index("dp")
    core = lax.axis_index("split")
    my, mz, mx = me // 16, me // 4 % 4, me % 4

    def peer(step, sign):
        y = (my + sign * step[0] + 4) % 4
        z = (mz + sign * step[1] + 4) % 4
        x = (mx + sign * step[2] + 4) % 4
        return (y * 16 + z * 4 + x, core)

    sibling = (me, 1 - core)

    def line(dim):
        return [peer([part if axis == dim else 0 for axis in range(3)], 1) for part in (1, 2, 3)]


    loads = [
        pltpu.make_async_copy(source, target, load_sem.at[index])
        for index, (source, target) in enumerate(
            ((cluster_hbm, cluster), (rank_hbm, rank), (emb_hbm, emb))
        )
    ]
    for load in loads:
        load.start()
    barrier = pltpu.get_barrier_semaphore()
    for dim in range(3):
        for target in line(dim):
            pl.semaphore_signal(barrier, inc=1, device_id=target, device_id_type=MESH)
    pl.semaphore_signal(barrier, inc=1, device_id=sibling, device_id_type=MESH)

    def greet(sem, dim):
        for target in line(dim):
            pl.semaphore_signal(sem, inc=1, device_id=target, device_id_type=MESH)

    loads[0].wait()
    loads[1].wait()
    slot = lax.broadcasted_iota(jnp.int32, (OWNERS, 128), 0)
    route = jnp.zeros((OWNERS, 128), jnp.int32)
    for index, step in enumerate(ORDER):
        route = jnp.where(slot == index, step[0] * 16 + step[1] * 4 + step[2], route)
    words = []
    for tile in range(8):
        ids = cluster[tile : tile + 1, :]
        owner = ids // 8
        step_y = (owner // 16 - my + 4) % 4
        step_z = (owner // 4 % 4 - mz + 4) % 4
        step_x = (owner % 4 - mx + 4) % 4
        code = step_y * 16 + step_z * 4 + step_x
        hit = jnp.where(route == code, 1.0, 0.0)
        hits[:, tile * 128 : (tile + 1) * 128] = hit.astype(jnp.bfloat16)
        words.append(ids % 8 * RANKS + rank[tile : tile + 1, :] + 1)
    lower = lax.broadcasted_iota(jnp.int32, (256, 256), 0)
    upper = lax.broadcasted_iota(jnp.int32, (256, 256), 1)
    before = jnp.where(lower <= upper, 1.0, 0.0).astype(jnp.bfloat16)
    carry = jnp.zeros((OWNERS, 1), jnp.float32)
    for part in range(4):
        cols = slice(part * 256, (part + 1) * 256)
        count = jnp.dot(hits[:, cols], before, preferred_element_type=jnp.float32) + carry
        carry = count[:, 255:256]
        place[:, cols] = jnp.where(hits[:, cols].astype(jnp.float32) > 0.5, count, 0.0)
    loads[2].wait()

    for start in range(0, ROWS, 128):
        values = emb[start : start + 128, :].astype(jnp.float32)
        total = jnp.sum(values * values, axis=1, keepdims=True)
        unit[start : start + 128, :] = (values * lax.rsqrt(total + 1e-06)).astype(jnp.bfloat16)

    leaving = [SLOT[code] for row in HOPS for code, _, first, _ in row if first]
    leaving.insert(GROUP * 2 - 1, 0)
    spot = lax.broadcasted_iota(jnp.int32, (CAP, ROWS), 0).astype(jnp.float32) + 1.0
    selected = []

    def select_until(count):
        while len(selected) < count:
            slots = leaving[len(selected) : len(selected) + GROUP]
            for index, slot in enumerate(slots):
                line = place[slot : slot + 1, :]
                chosen = jnp.where(jnp.broadcast_to(line, (CAP, ROWS)) == spot, 1.0, 0.0)
                sel[index * CAP : (index + 1) * CAP, :] = chosen.astype(jnp.bfloat16)
            picked = jnp.dot(sel[...], unit[...], preferred_element_type=jnp.float32)
            picked = picked.astype(jnp.bfloat16).reshape(GROUP, CAP, D)
            for index, slot in enumerate(slots):
                if slot == 0:
                    own_rows[0] = picked[index]
                else:
                    send_rows[slot] = picked[index]
            selected.extend(slots)

    def needed(number):
        slots = [SLOT[code] for row in HOPS[: number + 1] for code, _, first, _ in row if first]
        return max((leaving.index(slot) + 1 for slot in slots), default=0)

    def send_all_codes():
        turn = lax.broadcasted_iota(jnp.int32, (OWNERS, ROWS), 0) % 4 * CAP
        where = jnp.where(place[...] > 0.5, place[...] - 1.0 + turn.astype(jnp.float32), 0.0)
        where = jnp.sum(where, axis=0, keepdims=True)
        lane = lax.broadcasted_iota(jnp.int32, (128, ROWS), 0).astype(jnp.float32)
        picks[...] = jnp.where(lane == where, 1.0, 0.0).astype(jnp.bfloat16)

        word = jnp.concatenate(words, axis=1)
        codes = jnp.zeros((OWNERS, 128), jnp.float32)
        for power, digit in ((1, word % 256), (256, word // 256 % 256), (65536, word // 65536)):
            marked = hits[...] * digit.astype(jnp.float32).astype(jnp.bfloat16)
            codes = codes + nt_dot(marked, picks[...]) * float(power)
        send_codes[...] = codes.reshape(OWNERS, 1, 128)
        own_codes[0] = send_codes[0]
        for index in range(1, OWNERS):
            copy = pltpu.make_async_remote_copy(
                src_ref=send_codes.at[index], dst_ref=own_codes.at[index],
                send_sem=code_send, recv_sem=code_recv,
                device_id=peer(ORDER[index], 1), device_id_type=MESH,
            )
            copy.start()

    def spread(codes, keys, is_own):
        block = codes[...].reshape(OWNERS // 4, 4, 1, 128)
        line = jnp.sum(block, axis=1)
        if is_own:
            limits[0] = line
            limits[1] = jnp.floor((line - 1.0) * (1.0 / RANKS)) * float(RANKS) + 1.0
        line = jnp.where(line == 0.0, EMPTY, line)
        for index in range(OWNERS // 4):
            square = jnp.broadcast_to(line[index], (128, 128))
            keys[index * 128 : (index + 1) * 128, :] = square.T

    def compare(query, blocks):
        rows = own_rows[query * GROUP : (query + 1) * GROUP].reshape(WIDE, D)
        high = limits[0, query * 2 : query * 2 + 2]
        low = limits[1, query * 2 : query * 2 + 2]
        tops = [best[query, :, half * 128 : (half + 1) * 128] for half in range(2)]
        for is_far, block in blocks:
            data, keys = (far_rows, far_keys) if is_far else (own_rows, own_keys)
            scores = nt_dot(data[block * GROUP : (block + 1) * GROUP].reshape(WIDE, D), rows)
            code = keys[block * WIDE : (block + 1) * WIDE, :]
            for half in range(2):
                allowed = (code < high[half]) & (code >= low[half])
                part = scores[:, half * 128 : (half + 1) * 128]
                part = jnp.where(allowed, part, -1.0).reshape(WIDE // 8, 8, 128)
                tops[half] = jnp.maximum(tops[half], jnp.max(part, axis=0))
        for half in range(2):
            best[query, :, half * 128 : (half + 1) * 128] = tops[half]

    def finish():
        tops = jnp.max(best[...], axis=1)
        for query in range(GROUPS):
            for half in range(2):
                send_back[query * 2 + half] = tops[query : query + 1, half * 128 : (half + 1) * 128]
        got_back[0] = send_back[0]
        for index in sorted(range(1, OWNERS), key=lambda index: -hops_of(ORDER[index])):
            copy = pltpu.make_async_remote_copy(
                src_ref=send_back.at[index // 4], dst_ref=got_back.at[index],
                send_sem=back_send, recv_sem=back_recv,
                device_id=peer(ORDER[index], -1), device_id_type=MESH,
            )
            copy.start()

    best[...] = jnp.full(best.shape, -1.0, jnp.float32)
    queries, blocks, pairs, hops = [], [], [], []

    def compare_some(count):
        now = pairs[:count]
        del pairs[:count]
        while now:
            query = now[0][0]
            together = [block for other, block in now if other == query]
            now = [pair for pair in now if pair[0] != query]
            compare(query, together)

    def exchange(source, target, index):
        hop = pltpu.make_async_remote_copy(
            src_ref=source, dst_ref=target,
            send_sem=far_send.at[index], recv_sem=far_recv.at[index],
            device_id=sibling, device_id_type=MESH,
        )
        hop.start()
        hops.append(hop)
        return hop

    def codes_here():
        pltpu.make_async_copy(own_codes.at[1:], own_codes.at[1:], code_recv).wait()
        hop = exchange(own_codes, far_codes, GROUPS)
        spread(own_codes, own_keys, True)
        return lambda: codes_there(hop)

    def codes_there(hop):
        hop.wait_recv()
        spread(far_codes, far_keys, False)

    def group_here(group):
        here = own_rows.at[max(1, group * GROUP) : (group + 1) * GROUP]
        pltpu.make_async_copy(here, here, row_recv.at[group]).wait()
        rows = pl.ds(group * GROUP, GROUP)
        hop = exchange(own_rows.at[rows], far_rows.at[rows], group)
        pairs.extend((query, (False, group)) for query in queries)
        queries.append(group)
        blocks.append((False, group))
        pairs.extend((group, block) for block in blocks)
        return lambda: group_there(group, hop)

    def group_there(group, hop):
        hop.wait_recv()
        if group == GROUPS - 1:
            compare_some(len(pairs))
            for query in queries:
                compare(query, [(True, group)])
            finish()
            return
        blocks.append((True, group))
        pairs.extend((query, (True, group)) for query in queries)

    events, arrived = {}, 0
    for number, row in enumerate(HOPS):
        arrived += sum(last for _, _, _, last in row)
        for group in range(GROUPS):
            if arrived >= group * GROUP + GROUP - 1 and group not in events:
                events[group] = number + LAND
    todo = [(CODES_LAND, codes_here)]
    todo += [(max(CODES_LAND, events[group]), functools.partial(group_here, group)) for group in range(GROUPS)]
    parked, pass_at, number = {}, 0, 0
    select_until(needed(CODES_AT - 1))
    pl.semaphore_wait(barrier, 10)
    greet(plane_sem, 2)
    while number < len(HOPS) or todo or pairs:
        if number == PLANE_AT:
            pl.semaphore_wait(plane_sem, 3)
            greet(cube_sem, 1)
        if number == CODES_AT:
            pl.semaphore_wait(cube_sem, 3)
            send_all_codes()
        if number < len(HOPS):
            if number >= WAIT and number - WAIT in parked:
                here = transit.at[parked[number - WAIT]]
                pltpu.make_async_copy(here, here, pass_recv.at[number - WAIT]).wait()
            start = pass_at
            for code, dim, first, last in HOPS[number]:
                slot = SLOT[code]
                target = [0, 0, 0]
                target[dim] = step_of(code)[dim]
                if last:
                    place_there, arrival = own_rows.at[slot], row_recv.at[slot // GROUP]
                else:
                    place_there, arrival = transit.at[pass_at], pass_recv.at[number]
                copy = pltpu.make_async_remote_copy(
                    src_ref=send_rows.at[slot] if first else transit.at[parked[code, "at"]],
                    dst_ref=place_there,
                    send_sem=row_send if first else pass_send,
                    recv_sem=arrival,
                    device_id=peer(target, 1), device_id_type=MESH,
                )
                copy.start()
                if not last:
                    parked[code, "at"] = pass_at
                    pass_at += 1
            if pass_at > start:
                parked[number] = pl.ds(start, pass_at - start)
            select_until(needed(number + 2))
        for event in [event for event in todo if event[0] <= number]:
            todo.remove(event)
            following = event[1]()
            if following:
                todo.append((number + HOP, following))
        compare_some(PAIRS if number < len(HOPS) else LAST_PAIRS)
        number += 1

    pltpu.make_async_copy(got_back.at[1:], got_back.at[1:], back_recv).wait()
    back = got_back[...].reshape(OWNERS, 128)
    first = back.astype(jnp.bfloat16)
    rest = back - first.astype(jnp.float32)
    second = rest.astype(jnp.bfloat16)
    third = (rest - second.astype(jnp.float32)).astype(jnp.bfloat16)
    moved = jnp.dot(
        jnp.concatenate([first, second, third], axis=0), picks[...], preferred_element_type=jnp.float32
    )
    moved = moved[:OWNERS] + moved[OWNERS : 2 * OWNERS] + moved[2 * OWNERS :]
    result = jnp.sum(jnp.where(place[...] > 0.5, moved, 0.0), axis=0, keepdims=True)
    for tile in range(8):
        out_ref[tile : tile + 1, :] = result[:, tile * 128 : (tile + 1) * 128]

    pltpu.make_async_copy(send_rows.at[1:], send_rows.at[1:], row_send).wait()
    pltpu.make_async_copy(transit, transit, pass_send).wait()
    pltpu.make_async_copy(send_codes.at[1:], send_codes.at[1:], code_send).wait()
    pltpu.make_async_copy(got_back.at[1:], got_back.at[1:], back_send).wait()
    for hop in hops:
        hop.wait_send()


def shards(embeddings, cluster, rank):
    rows = (OWNERS, CAP, D)
    codes = (OWNERS, 1, 128)
    f32, bf16 = jnp.float32, jnp.bfloat16
    operands = (embeddings, cluster.reshape(8, 128), rank.reshape(8, 128))
    dma = pltpu.SemaphoreType.DMA
    result = pl.pallas_call(
        kernel,
        out_shape=jax.ShapeDtypeStruct((8, 128), f32),
        in_specs=[pl.BlockSpec(memory_space=pltpu.HBM)] * 3,
        out_specs=pl.BlockSpec(memory_space=pltpu.VMEM),
        scratch_shapes=[
            pltpu.VMEM((ROWS, D), bf16),
            pltpu.VMEM((8, 128), jnp.int32),
            pltpu.VMEM((8, 128), jnp.int32),
            pltpu.VMEM((ROWS, D), bf16),
            pltpu.VMEM((OWNERS, ROWS), bf16),
            pltpu.VMEM((OWNERS, ROWS), f32),
            pltpu.VMEM((WIDE, ROWS), bf16),
            pltpu.VMEM((128, ROWS), bf16),
            pltpu.VMEM(rows, bf16),
            pltpu.VMEM((TRANSITS, CAP, D), bf16),
            pltpu.VMEM(rows, bf16),
            pltpu.VMEM(rows, bf16),
            pltpu.VMEM(codes, f32),
            pltpu.VMEM(codes, f32),
            pltpu.VMEM(codes, f32),
            pltpu.VMEM((OWNERS * CAP, 128), f32),
            pltpu.VMEM((OWNERS * CAP, 128), f32),
            pltpu.VMEM((2, OWNERS // 4, 1, 128), f32),
            pltpu.VMEM((GROUPS, 8, WIDE), f32),
            pltpu.VMEM((OWNERS // 4, 1, 128), f32),
            pltpu.VMEM(codes, f32),
            dma((3,)),
            dma,
            dma,
            dma((len(HOPS),)),
            dma((GROUPS,)),
            dma,
            dma,
            dma((GROUPS + 1,)),
            dma((GROUPS + 1,)),
            dma,
            dma,
            pltpu.SemaphoreType.REGULAR,
            pltpu.SemaphoreType.REGULAR,
        ],
        compiler_params=pltpu.CompilerParams(
            collective_id=0, has_side_effects=True, vmem_limit_bytes=48 * 2**20
        ),
        cost_estimate=pl.CostEstimate(
            flops=2 * D * 2048 * (4096 + 1024), bytes_accessed=2 * ROWS * D, transcendentals=ROWS
        ),
        name="dedup",
    )(*(pltpu.with_memory_space_constraint(operand, pltpu.HBM) for operand in operands))
    return result.reshape(ROWS)


def solution(mesh):
    in_specs = (P(("dp", "split"), None), P(("dp", "split")), P(("dp", "split")))
    out_specs = P(("dp", "split"))
    return jax.shard_map(shards, mesh=mesh, in_specs=in_specs, out_specs=out_specs, check_vma=False)
```

```python
import functools

import jax
import jax.numpy as jnp
from jax import lax
from jax.experimental import pallas as pl
from jax.experimental.pallas import tpu as pltpu
from jax.sharding import PartitionSpec as P

MESH = pl.DeviceIdType.MESH
OWNERS = 64
CAP = 32
ROWS = 1024
D = 768
RANKS = 131072
GROUP = 8
GROUPS = OWNERS // GROUP
WIDE = GROUP * CAP
EMPTY = 16777216.0


PLAN = (
    (25, 5, 11, 96),
    (8, 48, 144, 13, 37),
    (111, 166, 91, 77, 83),
    (124, 140, 87, 183),
    (116, 60, 150, 16, 136),
    (108, 31, 161, 47),
    (163, 142, 53, 23, 69, 147),
    (92, 126, 76),
    (81, 165, 112, 184, 125, 131),
    (175, 152, 138),
    (17, 191, 114, 61, 46),
    (51, 162, 79, 32),
    (109, 88, 149, 143, 75, 159),
    (128, 123, 82),
    (90, 174, 22, 139, 113, 167),
    (130, 44, 135),
    (185, 71, 78, 189, 115, 187),
    (141, 172, 164),
    (160, 40, 89, 119, 66, 153),
    (176, 99, 127),
    (129, 19, 43, 137, 95),
    (178, 80, 63, 186),
    (173, 59, 72, 168, 70, 190),
    (117, 34, 68),
    (157, 85, 41, 155, 102),
    (20, 93, 180, 28),
    (54, 177, 64, 133, 188),
    (169, 101, 107, 120),
    (35, 57, 171, 73),
    (84, 156, 67, 104),
    (118, 94, 29),
    (65, 179, 132, 181),
    (105, 121, 56),
)
WAIT = 5
LAND = 5
PLANE_AT = 2
CODES_AT = 4
CODES_LAND = 9
HOP = 2
BOTH_FROM = 4
PAIRS = 7
LAST_PAIRS = 32


def step_of(code):
    return (code // 16, code // 4 % 4, code % 4)


def hops_of(step):
    return sum(min(part, 4 - part) for part in step)


def travel():
    hops, done, order = [], {}, [0]
    for entries in PLAN:
        row = []
        for entry in entries:
            code, dim = entry // 3, entry % 3
            passed = done.setdefault(code, set())
            first = not passed
            passed.add(dim)
            last = passed == {axis for axis, part in enumerate(step_of(code)) if part}
            if last:
                order.append(code)
            row.append((code, dim, first, last))
        hops.append(row)
    return hops, order


HOPS, ARRIVALS = travel()
ORDER = [step_of(code) for code in ARRIVALS]
SLOT = {code: slot for slot, code in enumerate(ARRIVALS)}
TRANSITS = sum(not last for row in HOPS for _, _, _, last in row)


def nt_dot(a, b):
    return lax.dot_general(a, b, (((1,), (1,)), ((), ())), preferred_element_type=jnp.float32)


def kernel(
    emb_hbm, cluster_hbm, rank_hbm, out_ref,
    emb, cluster, rank, unit, hits, place, sel, picks,
    send_rows, transit, own_rows, far_rows, send_codes, own_codes, far_codes,
    own_keys, far_keys, limits, best, send_back, got_back,
    load_sem, row_send, pass_send, pass_recv, row_recv, code_send, code_recv, far_send, far_recv, back_send, back_recv,
    plane_sem, cube_sem,
):
    me = lax.axis_index("dp")
    core = lax.axis_index("split")
    my, mz, mx = me // 16, me // 4 % 4, me % 4

    def peer(step, sign):
        y = (my + sign * step[0] + 4) % 4
        z = (mz + sign * step[1] + 4) % 4
        x = (mx + sign * step[2] + 4) % 4
        return (y * 16 + z * 4 + x, core)

    sibling = (me, 1 - core)

    def line(dim):
        return [peer([part if axis == dim else 0 for axis in range(3)], 1) for part in (1, 2, 3)]


    loads = [
        pltpu.make_async_copy(source, target, load_sem.at[index])
        for index, (source, target) in enumerate(
            ((cluster_hbm, cluster), (rank_hbm, rank), (emb_hbm, emb))
        )
    ]
    for load in loads:
        load.start()
    barrier = pltpu.get_barrier_semaphore()
    for dim in range(3):
        for target in line(dim):
            pl.semaphore_signal(barrier, inc=1, device_id=target, device_id_type=MESH)
    pl.semaphore_signal(barrier, inc=1, device_id=sibling, device_id_type=MESH)

    def greet(sem, dim):
        for target in line(dim):
            pl.semaphore_signal(sem, inc=1, device_id=target, device_id_type=MESH)

    loads[0].wait()
    loads[1].wait()
    slot = lax.broadcasted_iota(jnp.int32, (OWNERS, 128), 0)
    route = jnp.zeros((OWNERS, 128), jnp.int32)
    for index, step in enumerate(ORDER):
        route = jnp.where(slot == index, step[0] * 16 + step[1] * 4 + step[2], route)
    words = []
    for tile in range(8):
        ids = cluster[tile : tile + 1, :]
        owner = ids // 8
        step_y = (owner // 16 - my + 4) % 4
        step_z = (owner // 4 % 4 - mz + 4) % 4
        step_x = (owner % 4 - mx + 4) % 4
        code = step_y * 16 + step_z * 4 + step_x
        hit = jnp.where(route == code, 1.0, 0.0)
        hits[:, tile * 128 : (tile + 1) * 128] = hit.astype(jnp.bfloat16)
        words.append(ids % 8 * RANKS + rank[tile : tile + 1, :] + 1)
    lower = lax.broadcasted_iota(jnp.int32, (256, 256), 0)
    upper = lax.broadcasted_iota(jnp.int32, (256, 256), 1)
    before = jnp.where(lower <= upper, 1.0, 0.0).astype(jnp.bfloat16)
    carry = jnp.zeros((OWNERS, 1), jnp.float32)
    for part in range(4):
        cols = slice(part * 256, (part + 1) * 256)
        count = jnp.dot(hits[:, cols], before, preferred_element_type=jnp.float32) + carry
        carry = count[:, 255:256]
        place[:, cols] = jnp.where(hits[:, cols].astype(jnp.float32) > 0.5, count, 0.0)
    loads[2].wait()

    for start in range(0, ROWS, 128):
        values = emb[start : start + 128, :].astype(jnp.float32)
        total = jnp.sum(values * values, axis=1, keepdims=True)
        unit[start : start + 128, :] = (values * lax.rsqrt(total + 1e-06)).astype(jnp.bfloat16)

    leaving = [SLOT[code] for row in HOPS for code, _, first, _ in row if first]
    leaving.insert(GROUP * 2 - 1, 0)
    spot = lax.broadcasted_iota(jnp.int32, (CAP, ROWS), 0).astype(jnp.float32) + 1.0
    selected = []

    def select_until(count):
        while len(selected) < count:
            slots = leaving[len(selected) : len(selected) + GROUP]
            for index, slot in enumerate(slots):
                line = place[slot : slot + 1, :]
                chosen = jnp.where(jnp.broadcast_to(line, (CAP, ROWS)) == spot, 1.0, 0.0)
                sel[index * CAP : (index + 1) * CAP, :] = chosen.astype(jnp.bfloat16)
            picked = jnp.dot(sel[...], unit[...], preferred_element_type=jnp.float32)
            picked = picked.astype(jnp.bfloat16).reshape(GROUP, CAP, D)
            for index, slot in enumerate(slots):
                if slot == 0:
                    own_rows[0] = picked[index]
                else:
                    send_rows[slot] = picked[index]
            selected.extend(slots)

    def needed(number):
        slots = [SLOT[code] for row in HOPS[: number + 1] for code, _, first, _ in row if first]
        return max((leaving.index(slot) + 1 for slot in slots), default=0)

    def send_all_codes():
        turn = lax.broadcasted_iota(jnp.int32, (OWNERS, ROWS), 0) % 4 * CAP
        where = jnp.where(place[...] > 0.5, place[...] - 1.0 + turn.astype(jnp.float32), 0.0)
        where = jnp.sum(where, axis=0, keepdims=True)
        lane = lax.broadcasted_iota(jnp.int32, (128, ROWS), 0).astype(jnp.float32)
        picks[...] = jnp.where(lane == where, 1.0, 0.0).astype(jnp.bfloat16)

        word = jnp.concatenate(words, axis=1)
        codes = jnp.zeros((OWNERS, 128), jnp.float32)
        for power, digit in ((1, word % 256), (256, word // 256 % 256), (65536, word // 65536)):
            marked = hits[...] * digit.astype(jnp.float32).astype(jnp.bfloat16)
            codes = codes + nt_dot(marked, picks[...]) * float(power)
        send_codes[...] = codes.reshape(OWNERS, 1, 128)
        own_codes[0] = send_codes[0]
        for index in range(1, OWNERS):
            copy = pltpu.make_async_remote_copy(
                src_ref=send_codes.at[index], dst_ref=own_codes.at[index],
                send_sem=code_send, recv_sem=code_recv,
                device_id=peer(ORDER[index], 1), device_id_type=MESH,
            )
            copy.start()

    def spread(codes, keys, is_own):
        block = codes[...].reshape(OWNERS // 4, 4, 1, 128)
        line = jnp.sum(block, axis=1)
        if is_own:
            limits[0] = line
            limits[1] = jnp.floor((line - 1.0) * (1.0 / RANKS)) * float(RANKS) + 1.0
        line = jnp.where(line == 0.0, EMPTY, line)
        for index in range(OWNERS // 4):
            square = jnp.broadcast_to(line[index], (128, 128))
            keys[index * 128 : (index + 1) * 128, :] = square.T

    def compare_back(scores, code, high, block):
        base = jnp.floor((code - 1.0) * (1.0 / RANKS)) * float(RANKS) + 1.0
        top = None
        for half in range(2):
            key = jnp.where(high[half] == 0.0, EMPTY, high[half])
            part = scores[:, half * 128 : (half + 1) * 128]
            part = jnp.where((key < code) & (key >= base), part, -1.0)
            top = part if top is None else jnp.maximum(top, part)
        for half in range(2):
            cols = slice(half * 128, (half + 1) * 128)
            line = jnp.max(top[cols, :].T, axis=0, keepdims=True)
            best[block, 0:1, cols] = jnp.maximum(best[block, 0:1, cols], line)

    def compare(query, blocks):
        rows = own_rows[query * GROUP : (query + 1) * GROUP].reshape(WIDE, D)
        high = limits[0, query * 2 : query * 2 + 2]
        low = limits[1, query * 2 : query * 2 + 2]
        tops = [best[query, :, half * 128 : (half + 1) * 128] for half in range(2)]
        for is_far, block in blocks:
            data, keys = (far_rows, far_keys) if is_far else (own_rows, own_keys)
            scores = nt_dot(data[block * GROUP : (block + 1) * GROUP].reshape(WIDE, D), rows)
            code = keys[block * WIDE : (block + 1) * WIDE, :]
            for half in range(2):
                allowed = (code < high[half]) & (code >= low[half])
                part = scores[:, half * 128 : (half + 1) * 128]
                part = jnp.where(allowed, part, -1.0).reshape(WIDE // 8, 8, 128)
                tops[half] = jnp.maximum(tops[half], jnp.max(part, axis=0))
            if is_far is None:
                compare_back(scores, code, high, block)
        for half in range(2):
            best[query, :, half * 128 : (half + 1) * 128] = tops[half]

    def finish():
        tops = jnp.max(best[...], axis=1)
        for query in range(GROUPS):
            for half in range(2):
                send_back[query * 2 + half] = tops[query : query + 1, half * 128 : (half + 1) * 128]
        got_back[0] = send_back[0]
        for index in sorted(range(1, OWNERS), key=lambda index: -hops_of(ORDER[index])):
            copy = pltpu.make_async_remote_copy(
                src_ref=send_back.at[index // 4], dst_ref=got_back.at[index],
                send_sem=back_send, recv_sem=back_recv,
                device_id=peer(ORDER[index], -1), device_id_type=MESH,
            )
            copy.start()

    best[...] = jnp.full(best.shape, -1.0, jnp.float32)
    queries, blocks, pairs, hops = [], [], [], []

    def compare_some(count):
        now = pairs[:count]
        del pairs[:count]
        while now:
            query = now[0][0]
            together = [block for other, block in now if other == query]
            now = [pair for pair in now if pair[0] != query]
            compare(query, together)

    def exchange(source, target, index):
        hop = pltpu.make_async_remote_copy(
            src_ref=source, dst_ref=target,
            send_sem=far_send.at[index], recv_sem=far_recv.at[index],
            device_id=sibling, device_id_type=MESH,
        )
        hop.start()
        hops.append(hop)
        return hop

    def codes_here():
        pltpu.make_async_copy(own_codes.at[1:], own_codes.at[1:], code_recv).wait()
        hop = exchange(own_codes, far_codes, GROUPS)
        spread(own_codes, own_keys, True)
        return lambda: codes_there(hop)

    def codes_there(hop):
        hop.wait_recv()
        spread(far_codes, far_keys, False)

    def group_here(group):
        here = own_rows.at[max(1, group * GROUP) : (group + 1) * GROUP]
        pltpu.make_async_copy(here, here, row_recv.at[group]).wait()
        rows = pl.ds(group * GROUP, GROUP)
        hop = exchange(own_rows.at[rows], far_rows.at[rows], group)
        if group < BOTH_FROM:
            pairs.extend((query, (False, group)) for query in queries)
        queries.append(group)
        blocks.append((False, group))
        for is_far, block in blocks:
            both = group >= BOTH_FROM and not is_far and block != group
            pairs.append((group, (None if both else is_far, block)))
        return lambda: group_there(group, hop)

    def group_there(group, hop):
        hop.wait_recv()
        if group == GROUPS - 1:
            compare_some(len(pairs))
            for query in queries:
                compare(query, [(True, group)])
            finish()
            return
        blocks.append((True, group))
        pairs.extend((query, (True, group)) for query in queries)

    events, arrived = {}, 0
    for number, row in enumerate(HOPS):
        arrived += sum(last for _, _, _, last in row)
        for group in range(GROUPS):
            if arrived >= group * GROUP + GROUP - 1 and group not in events:
                events[group] = number + LAND
    todo = [(CODES_LAND, codes_here)]
    todo += [(max(CODES_LAND, events[group]), functools.partial(group_here, group)) for group in range(GROUPS)]
    parked, pass_at, number = {}, 0, 0
    select_until(needed(CODES_AT - 1))
    pl.semaphore_wait(barrier, 10)
    greet(plane_sem, 2)
    while number < len(HOPS) or todo or pairs:
        if number == PLANE_AT:
            pl.semaphore_wait(plane_sem, 3)
            greet(cube_sem, 1)
        if number == CODES_AT:
            pl.semaphore_wait(cube_sem, 3)
            send_all_codes()
        if number < len(HOPS):
            if number >= WAIT and number - WAIT in parked:
                here = transit.at[parked[number - WAIT]]
                pltpu.make_async_copy(here, here, pass_recv.at[number - WAIT]).wait()
            start = pass_at
            for code, dim, first, last in HOPS[number]:
                slot = SLOT[code]
                target = [0, 0, 0]
                target[dim] = step_of(code)[dim]
                if last:
                    place_there, arrival = own_rows.at[slot], row_recv.at[slot // GROUP]
                else:
                    place_there, arrival = transit.at[pass_at], pass_recv.at[number]
                copy = pltpu.make_async_remote_copy(
                    src_ref=send_rows.at[slot] if first else transit.at[parked[code, "at"]],
                    dst_ref=place_there,
                    send_sem=row_send if first else pass_send,
                    recv_sem=arrival,
                    device_id=peer(target, 1), device_id_type=MESH,
                )
                copy.start()
                if not last:
                    parked[code, "at"] = pass_at
                    pass_at += 1
            if pass_at > start:
                parked[number] = pl.ds(start, pass_at - start)
            select_until(needed(number + 2))
        for event in [event for event in todo if event[0] <= number]:
            todo.remove(event)
            following = event[1]()
            if following:
                todo.append((number + (HOP if number < len(HOPS) else 1), following))
        compare_some(PAIRS if number < len(HOPS) else LAST_PAIRS)
        number += 1

    pltpu.make_async_copy(got_back.at[1:], got_back.at[1:], back_recv).wait()
    back = got_back[...].reshape(OWNERS, 128)
    first = back.astype(jnp.bfloat16)
    rest = back - first.astype(jnp.float32)
    second = rest.astype(jnp.bfloat16)
    third = (rest - second.astype(jnp.float32)).astype(jnp.bfloat16)
    moved = jnp.dot(
        jnp.concatenate([first, second, third], axis=0), picks[...], preferred_element_type=jnp.float32
    )
    moved = moved[:OWNERS] + moved[OWNERS : 2 * OWNERS] + moved[2 * OWNERS :]
    result = jnp.sum(jnp.where(place[...] > 0.5, moved, 0.0), axis=0, keepdims=True)
    for tile in range(8):
        out_ref[tile : tile + 1, :] = result[:, tile * 128 : (tile + 1) * 128]

    pltpu.make_async_copy(send_rows.at[1:], send_rows.at[1:], row_send).wait()
    pltpu.make_async_copy(transit, transit, pass_send).wait()
    pltpu.make_async_copy(send_codes.at[1:], send_codes.at[1:], code_send).wait()
    pltpu.make_async_copy(got_back.at[1:], got_back.at[1:], back_send).wait()
    for hop in hops:
        hop.wait_send()


def shards(embeddings, cluster, rank):
    rows = (OWNERS, CAP, D)
    codes = (OWNERS, 1, 128)
    f32, bf16 = jnp.float32, jnp.bfloat16
    operands = (embeddings, cluster.reshape(8, 128), rank.reshape(8, 128))
    dma = pltpu.SemaphoreType.DMA
    result = pl.pallas_call(
        kernel,
        out_shape=jax.ShapeDtypeStruct((8, 128), f32),
        in_specs=[pl.BlockSpec(memory_space=pltpu.HBM)] * 3,
        out_specs=pl.BlockSpec(memory_space=pltpu.VMEM),
        scratch_shapes=[
            pltpu.VMEM((ROWS, D), bf16),
            pltpu.VMEM((8, 128), jnp.int32),
            pltpu.VMEM((8, 128), jnp.int32),
            pltpu.VMEM((ROWS, D), bf16),
            pltpu.VMEM((OWNERS, ROWS), bf16),
            pltpu.VMEM((OWNERS, ROWS), f32),
            pltpu.VMEM((WIDE, ROWS), bf16),
            pltpu.VMEM((128, ROWS), bf16),
            pltpu.VMEM(rows, bf16),
            pltpu.VMEM((TRANSITS, CAP, D), bf16),
            pltpu.VMEM(rows, bf16),
            pltpu.VMEM(rows, bf16),
            pltpu.VMEM(codes, f32),
            pltpu.VMEM(codes, f32),
            pltpu.VMEM(codes, f32),
            pltpu.VMEM((OWNERS * CAP, 128), f32),
            pltpu.VMEM((OWNERS * CAP, 128), f32),
            pltpu.VMEM((2, OWNERS // 4, 1, 128), f32),
            pltpu.VMEM((GROUPS, 8, WIDE), f32),
            pltpu.VMEM((OWNERS // 4, 1, 128), f32),
            pltpu.VMEM(codes, f32),
            dma((3,)),
            dma,
            dma,
            dma((len(HOPS),)),
            dma((GROUPS,)),
            dma,
            dma,
            dma((GROUPS + 1,)),
            dma((GROUPS + 1,)),
            dma,
            dma,
            pltpu.SemaphoreType.REGULAR,
            pltpu.SemaphoreType.REGULAR,
        ],
        compiler_params=pltpu.CompilerParams(
            collective_id=0, has_side_effects=True, vmem_limit_bytes=48 * 2**20
        ),
        cost_estimate=pl.CostEstimate(
            flops=2 * D * 2048 * (4096 + 1024), bytes_accessed=2 * ROWS * D, transcendentals=ROWS
        ),
        name="dedup",
    )(*(pltpu.with_memory_space_constraint(operand, pltpu.HBM) for operand in operands))
    return result.reshape(ROWS)


def solution(mesh):
    in_specs = (P(("dp", "split"), None), P(("dp", "split")), P(("dp", "split")))
    out_specs = P(("dp", "split"))
    return jax.shard_map(shards, mesh=mesh, in_specs=in_specs, out_specs=out_specs, check_vma=False)
```

```python
import functools

import jax
import jax.numpy as jnp
from jax import lax
from jax.experimental import pallas as pl
from jax.experimental.pallas import tpu as pltpu
from jax.sharding import PartitionSpec as P

MESH = pl.DeviceIdType.MESH
OWNERS = 64
CAP = 32
ROWS = 1024
D = 768
RANKS = 131072
GROUP = 8
GROUPS = OWNERS // GROUP
WIDE = GROUP * CAP
EMPTY = 16777216.0


PLAN = (
    (25, 5, 11, 96),
    (8, 48, 144, 13, 37),
    (111, 166, 91, 77, 83),
    (124, 140, 87, 183),
    (116, 60, 150, 16, 136),
    (108, 31, 161, 47),
    (163, 142, 53, 23, 69, 147),
    (92, 126, 76),
    (81, 165, 112, 184, 125, 131),
    (175, 152, 138),
    (17, 191, 114, 61, 46),
    (51, 162, 79, 32),
    (109, 88, 149, 143, 75, 159),
    (128, 123, 82),
    (90, 174, 22, 139, 113, 167),
    (130, 44, 135),
    (185, 71, 78, 189, 115, 187),
    (141, 172, 164),
    (160, 40, 89, 119, 66, 153),
    (176, 99, 127),
    (129, 19, 43, 137, 95),
    (178, 80, 63, 186),
    (173, 59, 72, 168, 70, 190),
    (117, 34, 68),
    (157, 85, 41, 155, 102),
    (20, 93, 180, 28),
    (54, 177, 64, 133, 188),
    (169, 101, 107, 120),
    (35, 57, 171, 73),
    (84, 156, 67, 104),
    (118, 94, 29),
    (65, 179, 132, 181),
    (105, 121, 56),
)
WAIT = 5
LAND = 5
PLANE_AT = 2
CODES_AT = 4
CODES_LAND = 9
HOP = 2
BOTH_FROM = 4
PAIRS = 7
LAST_PAIRS = 32


def step_of(code):
    return (code // 16, code // 4 % 4, code % 4)


def hops_of(step):
    return sum(min(part, 4 - part) for part in step)


def travel():
    hops, done, order = [], {}, [0]
    for entries in PLAN:
        row = []
        for entry in entries:
            code, dim = entry // 3, entry % 3
            passed = done.setdefault(code, set())
            first = not passed
            passed.add(dim)
            last = passed == {axis for axis, part in enumerate(step_of(code)) if part}
            if last:
                order.append(code)
            row.append((code, dim, first, last))
        hops.append(row)
    return hops, order


HOPS, ARRIVALS = travel()
ORDER = [step_of(code) for code in ARRIVALS]
SLOT = {code: slot for slot, code in enumerate(ARRIVALS)}
TRANSITS = sum(not last for row in HOPS for _, _, _, last in row)


def nt_dot(a, b):
    return lax.dot_general(a, b, (((1,), (1,)), ((), ())), preferred_element_type=jnp.float32)


def kernel(
    emb_hbm, cluster_hbm, rank_hbm, out_ref,
    emb, cluster, rank, unit, hits, place, sel, picks,
    send_rows, transit, own_rows, far_rows, send_codes, own_codes, far_codes,
    own_keys, far_keys, limits, best, send_back, got_back,
    load_sem, row_send, pass_send, pass_recv, row_recv, code_send, code_recv, far_send, far_recv, back_send, back_recv,
    plane_sem, cube_sem,
):
    me = lax.axis_index("dp")
    core = lax.axis_index("split")
    my, mz, mx = me // 16, me // 4 % 4, me % 4

    def peer(step, sign):
        y = (my + sign * step[0] + 4) % 4
        z = (mz + sign * step[1] + 4) % 4
        x = (mx + sign * step[2] + 4) % 4
        return (y * 16 + z * 4 + x, core)

    sibling = (me, 1 - core)

    def line(dim):
        return [peer([part if axis == dim else 0 for axis in range(3)], 1) for part in (1, 2, 3)]


    loads = [
        pltpu.make_async_copy(source, target, load_sem.at[index])
        for index, (source, target) in enumerate(
            ((cluster_hbm, cluster), (rank_hbm, rank), (emb_hbm, emb))
        )
    ]
    for load in loads:
        load.start()
    barrier = pltpu.get_barrier_semaphore()
    for dim in range(3):
        for target in line(dim):
            pl.semaphore_signal(barrier, inc=1, device_id=target, device_id_type=MESH)
    pl.semaphore_signal(barrier, inc=1, device_id=sibling, device_id_type=MESH)

    def greet(sem, dim):
        for target in line(dim):
            pl.semaphore_signal(sem, inc=1, device_id=target, device_id_type=MESH)

    loads[0].wait()
    loads[1].wait()
    slot = lax.broadcasted_iota(jnp.int32, (OWNERS, 128), 0)
    route = jnp.zeros((OWNERS, 128), jnp.int32)
    for index, step in enumerate(ORDER):
        route = jnp.where(slot == index, step[0] * 16 + step[1] * 4 + step[2], route)
    words = []
    for tile in range(8):
        ids = cluster[tile : tile + 1, :]
        owner = ids // 8
        step_y = (owner // 16 - my + 4) % 4
        step_z = (owner // 4 % 4 - mz + 4) % 4
        step_x = (owner % 4 - mx + 4) % 4
        code = step_y * 16 + step_z * 4 + step_x
        hit = jnp.where(route == code, 1.0, 0.0)
        hits[:, tile * 128 : (tile + 1) * 128] = hit.astype(jnp.bfloat16)
        words.append(ids % 8 * RANKS + rank[tile : tile + 1, :] + 1)
    lower = lax.broadcasted_iota(jnp.int32, (256, 256), 0)
    upper = lax.broadcasted_iota(jnp.int32, (256, 256), 1)
    before = jnp.where(lower <= upper, 1.0, 0.0).astype(jnp.bfloat16)
    carry = jnp.zeros((OWNERS, 1), jnp.float32)
    for part in range(4):
        cols = slice(part * 256, (part + 1) * 256)
        count = jnp.dot(hits[:, cols], before, preferred_element_type=jnp.float32) + carry
        carry = count[:, 255:256]
        place[:, cols] = jnp.where(hits[:, cols].astype(jnp.float32) > 0.5, count, 0.0)
    loads[2].wait()

    for start in range(0, ROWS, 128):
        values = emb[start : start + 128, :].astype(jnp.float32)
        total = jnp.sum(values * values, axis=1, keepdims=True)
        unit[start : start + 128, :] = (values * lax.rsqrt(total + 1e-06)).astype(jnp.bfloat16)

    leaving = [SLOT[code] for row in HOPS for code, _, first, _ in row if first]
    leaving.insert(GROUP * 2 - 1, 0)
    spot = lax.broadcasted_iota(jnp.int32, (CAP, ROWS), 0).astype(jnp.float32) + 1.0
    selected = []

    def select_until(count):
        while len(selected) < count:
            slots = leaving[len(selected) : len(selected) + GROUP]
            for index, slot in enumerate(slots):
                line = place[slot : slot + 1, :]
                chosen = jnp.where(jnp.broadcast_to(line, (CAP, ROWS)) == spot, 1.0, 0.0)
                sel[index * CAP : (index + 1) * CAP, :] = chosen.astype(jnp.bfloat16)
            picked = jnp.dot(sel[...], unit[...], preferred_element_type=jnp.float32)
            picked = picked.astype(jnp.bfloat16).reshape(GROUP, CAP, D)
            for index, slot in enumerate(slots):
                if slot == 0:
                    own_rows[0] = picked[index]
                else:
                    send_rows[slot] = picked[index]
            selected.extend(slots)

    def needed(number):
        slots = [SLOT[code] for row in HOPS[: number + 1] for code, _, first, _ in row if first]
        return max((leaving.index(slot) + 1 for slot in slots), default=0)

    def send_all_codes():
        turn = lax.broadcasted_iota(jnp.int32, (OWNERS, ROWS), 0) % 4 * CAP
        where = jnp.where(place[...] > 0.5, place[...] - 1.0 + turn.astype(jnp.float32), 0.0)
        where = jnp.sum(where, axis=0, keepdims=True)
        lane = lax.broadcasted_iota(jnp.int32, (128, ROWS), 0).astype(jnp.float32)
        picks[...] = jnp.where(lane == where, 1.0, 0.0).astype(jnp.bfloat16)

        word = jnp.concatenate(words, axis=1)
        codes = jnp.zeros((OWNERS, 128), jnp.float32)
        for power, digit in ((1, word % 256), (256, word // 256 % 256), (65536, word // 65536)):
            marked = hits[...] * digit.astype(jnp.float32).astype(jnp.bfloat16)
            codes = codes + nt_dot(marked, picks[...]) * float(power)
        send_codes[...] = codes.reshape(OWNERS, 1, 128)
        own_codes[0] = send_codes[0]
        for index in range(1, OWNERS):
            copy = pltpu.make_async_remote_copy(
                src_ref=send_codes.at[index], dst_ref=own_codes.at[index],
                send_sem=code_send, recv_sem=code_recv,
                device_id=peer(ORDER[index], 1), device_id_type=MESH,
            )
            copy.start()

    def spread(codes, keys, is_own):
        block = codes[...].reshape(OWNERS // 4, 4, 1, 128)
        line = jnp.sum(block, axis=1)
        if is_own:
            limits[0] = line
            limits[1] = jnp.floor((line - 1.0) * (1.0 / RANKS)) * float(RANKS) + 1.0
        line = jnp.where(line == 0.0, EMPTY, line)
        for index in range(OWNERS // 4):
            square = jnp.broadcast_to(line[index], (128, 128))
            keys[index * 128 : (index + 1) * 128, :] = square.T

    def compare_back(scores, code, high, block):
        base = jnp.floor((code - 1.0) * (1.0 / RANKS)) * float(RANKS) + 1.0
        top = None
        for half in range(2):
            key = jnp.where(high[half] == 0.0, EMPTY, high[half])
            part = scores[:, half * 128 : (half + 1) * 128]
            part = jnp.where((key < code) & (key >= base), part, -1.0)
            top = part if top is None else jnp.maximum(top, part)
        for half in range(2):
            cols = slice(half * 128, (half + 1) * 128)
            line = jnp.max(top[cols, :].T, axis=0, keepdims=True)
            best[block, 0:1, cols] = jnp.maximum(best[block, 0:1, cols], line)

    def compare(query, blocks):
        rows = own_rows[query * GROUP : (query + 1) * GROUP].reshape(WIDE, D)
        high = limits[0, query * 2 : query * 2 + 2]
        low = limits[1, query * 2 : query * 2 + 2]
        tops = [best[query, :, half * 128 : (half + 1) * 128] for half in range(2)]
        for is_far, block in blocks:
            data, keys = (far_rows, far_keys) if is_far else (own_rows, own_keys)
            scores = nt_dot(data[block * GROUP : (block + 1) * GROUP].reshape(WIDE, D), rows)
            code = keys[block * WIDE : (block + 1) * WIDE, :]
            for half in range(2):
                allowed = (code < high[half]) & (code >= low[half])
                part = scores[:, half * 128 : (half + 1) * 128]
                part = jnp.where(allowed, part, -1.0).reshape(WIDE // 8, 8, 128)
                tops[half] = jnp.maximum(tops[half], jnp.max(part, axis=0))
            if is_far is None:
                compare_back(scores, code, high, block)
        for half in range(2):
            best[query, :, half * 128 : (half + 1) * 128] = tops[half]

    def finish():
        tops = jnp.max(best[...], axis=1)
        for query in range(GROUPS):
            for half in range(2):
                send_back[query * 2 + half] = tops[query : query + 1, half * 128 : (half + 1) * 128]
        got_back[0] = send_back[0]
        for index in sorted(range(1, OWNERS), key=lambda index: -hops_of(ORDER[index])):
            copy = pltpu.make_async_remote_copy(
                src_ref=send_back.at[index // 4], dst_ref=got_back.at[index],
                send_sem=back_send, recv_sem=back_recv,
                device_id=peer(ORDER[index], -1), device_id_type=MESH,
            )
            copy.start()

    best[...] = jnp.full(best.shape, -1.0, jnp.float32)
    queries, blocks, pairs, hops = [], [], [], []

    def compare_some(count):
        now = pairs[:count]
        del pairs[:count]
        while now:
            query = now[0][0]
            together = [block for other, block in now if other == query]
            now = [pair for pair in now if pair[0] != query]
            compare(query, together)

    def exchange(source, target, index):
        hop = pltpu.make_async_remote_copy(
            src_ref=source, dst_ref=target,
            send_sem=far_send.at[index], recv_sem=far_recv.at[index],
            device_id=sibling, device_id_type=MESH,
        )
        hop.start()
        hops.append(hop)
        return hop

    def codes_here():
        pltpu.make_async_copy(own_codes.at[1:], own_codes.at[1:], code_recv).wait()
        hop = exchange(own_codes, far_codes, GROUPS)
        spread(own_codes, own_keys, True)
        return lambda: codes_there(hop)

    def codes_there(hop):
        hop.wait_recv()
        spread(far_codes, far_keys, False)

    def group_here(group):
        here = own_rows.at[max(1, group * GROUP) : (group + 1) * GROUP]
        pltpu.make_async_copy(here, here, row_recv.at[group]).wait()
        rows = pl.ds(group * GROUP, GROUP)
        hop = exchange(own_rows.at[rows], far_rows.at[rows], group)
        if group < BOTH_FROM:
            pairs.extend((query, (False, group)) for query in queries)
        queries.append(group)
        blocks.append((False, group))
        for is_far, block in blocks:
            both = group >= BOTH_FROM and not is_far and block != group
            pairs.append((group, (None if both else is_far, block)))
        return lambda: group_there(group, hop)

    def group_there(group, hop):
        hop.wait_recv()
        if group == GROUPS - 1:
            compare_some(len(pairs))
            for query in queries:
                compare(query, [(True, group)])
            finish()
            return
        blocks.append((True, group))
        pairs.extend((query, (True, group)) for query in queries)

    events, arrived = {}, 0
    for number, row in enumerate(HOPS):
        arrived += sum(last for _, _, _, last in row)
        for group in range(GROUPS):
            if arrived >= group * GROUP + GROUP - 1 and group not in events:
                events[group] = number + LAND
    todo = [(CODES_LAND, codes_here)]
    todo += [(max(CODES_LAND, events[group]), functools.partial(group_here, group)) for group in range(GROUPS)]
    parked, pass_at, number = {}, 0, 0
    select_until(needed(CODES_AT - 1))
    pl.semaphore_wait(barrier, 10)
    greet(plane_sem, 2)
    while number < len(HOPS) or todo or pairs:
        if number == PLANE_AT:
            pl.semaphore_wait(plane_sem, 3)
            greet(cube_sem, 1)
        if number == CODES_AT:
            pl.semaphore_wait(cube_sem, 3)
            send_all_codes()
        if number < len(HOPS):
            if number >= WAIT and number - WAIT in parked:
                here = transit.at[parked[number - WAIT]]
                pltpu.make_async_copy(here, here, pass_recv.at[number - WAIT]).wait()
            start = pass_at
            for code, dim, first, last in HOPS[number]:
                slot = SLOT[code]
                target = [0, 0, 0]
                target[dim] = step_of(code)[dim]
                if last:
                    place_there, arrival = own_rows.at[slot], row_recv.at[slot // GROUP]
                else:
                    place_there, arrival = transit.at[pass_at], pass_recv.at[number]
                copy = pltpu.make_async_remote_copy(
                    src_ref=send_rows.at[slot] if first else transit.at[parked[code, "at"]],
                    dst_ref=place_there,
                    send_sem=row_send if first else pass_send,
                    recv_sem=arrival,
                    device_id=peer(target, 1), device_id_type=MESH,
                )
                copy.start()
                if not last:
                    parked[code, "at"] = pass_at
                    pass_at += 1
            if pass_at > start:
                parked[number] = pl.ds(start, pass_at - start)
            select_until(needed(number + 2))
        for event in [event for event in todo if event[0] <= number]:
            todo.remove(event)
            following = event[1]()
            if following:
                todo.append((number + HOP, following))
        compare_some(PAIRS if number < len(HOPS) else LAST_PAIRS)
        number += 1

    pltpu.make_async_copy(got_back.at[1:], got_back.at[1:], back_recv).wait()
    back = got_back[...].reshape(OWNERS, 128)
    first = back.astype(jnp.bfloat16)
    rest = back - first.astype(jnp.float32)
    second = rest.astype(jnp.bfloat16)
    third = (rest - second.astype(jnp.float32)).astype(jnp.bfloat16)
    moved = jnp.dot(
        jnp.concatenate([first, second, third], axis=0), picks[...], preferred_element_type=jnp.float32
    )
    moved = moved[:OWNERS] + moved[OWNERS : 2 * OWNERS] + moved[2 * OWNERS :]
    result = jnp.sum(jnp.where(place[...] > 0.5, moved, 0.0), axis=0, keepdims=True)
    for tile in range(8):
        out_ref[tile : tile + 1, :] = result[:, tile * 128 : (tile + 1) * 128]

    pltpu.make_async_copy(send_rows.at[1:], send_rows.at[1:], row_send).wait()
    pltpu.make_async_copy(transit, transit, pass_send).wait()
    pltpu.make_async_copy(send_codes.at[1:], send_codes.at[1:], code_send).wait()
    pltpu.make_async_copy(got_back.at[1:], got_back.at[1:], back_send).wait()
    for hop in hops:
        hop.wait_send()


def shards(embeddings, cluster, rank):
    rows = (OWNERS, CAP, D)
    codes = (OWNERS, 1, 128)
    f32, bf16 = jnp.float32, jnp.bfloat16
    operands = (embeddings, cluster.reshape(8, 128), rank.reshape(8, 128))
    dma = pltpu.SemaphoreType.DMA
    result = pl.pallas_call(
        kernel,
        out_shape=jax.ShapeDtypeStruct((8, 128), f32),
        in_specs=[pl.BlockSpec(memory_space=pltpu.HBM)] * 3,
        out_specs=pl.BlockSpec(memory_space=pltpu.VMEM),
        scratch_shapes=[
            pltpu.VMEM((ROWS, D), bf16),
            pltpu.VMEM((8, 128), jnp.int32),
            pltpu.VMEM((8, 128), jnp.int32),
            pltpu.VMEM((ROWS, D), bf16),
            pltpu.VMEM((OWNERS, ROWS), bf16),
            pltpu.VMEM((OWNERS, ROWS), f32),
            pltpu.VMEM((WIDE, ROWS), bf16),
            pltpu.VMEM((128, ROWS), bf16),
            pltpu.VMEM(rows, bf16),
            pltpu.VMEM((TRANSITS, CAP, D), bf16),
            pltpu.VMEM(rows, bf16),
            pltpu.VMEM(rows, bf16),
            pltpu.VMEM(codes, f32),
            pltpu.VMEM(codes, f32),
            pltpu.VMEM(codes, f32),
            pltpu.VMEM((OWNERS * CAP, 128), f32),
            pltpu.VMEM((OWNERS * CAP, 128), f32),
            pltpu.VMEM((2, OWNERS // 4, 1, 128), f32),
            pltpu.VMEM((GROUPS, 8, WIDE), f32),
            pltpu.VMEM((OWNERS // 4, 1, 128), f32),
            pltpu.VMEM(codes, f32),
            dma((3,)),
            dma,
            dma,
            dma((len(HOPS),)),
            dma((GROUPS,)),
            dma,
            dma,
            dma((GROUPS + 1,)),
            dma((GROUPS + 1,)),
            dma,
            dma,
            pltpu.SemaphoreType.REGULAR,
            pltpu.SemaphoreType.REGULAR,
        ],
        compiler_params=pltpu.CompilerParams(
            collective_id=0, has_side_effects=True, vmem_limit_bytes=48 * 2**20
        ),
        cost_estimate=pl.CostEstimate(
            flops=2 * D * 2048 * (4096 + 1024), bytes_accessed=2 * ROWS * D, transcendentals=ROWS
        ),
        name="dedup",
    )(*(pltpu.with_memory_space_constraint(operand, pltpu.HBM) for operand in operands))
    return result.reshape(ROWS)


def solution(mesh):
    in_specs = (P(("dp", "split"), None), P(("dp", "split")), P(("dp", "split")))
    out_specs = P(("dp", "split"))
    return jax.shard_map(shards, mesh=mesh, in_specs=in_specs, out_specs=out_specs, check_vma=False)
```
